32 devices in a mesh: dp: 16 (over z, x, core), tensor: 2 (over y).
Axes of the slice: x: 2, y: 2, z: 4, core: 2. Of those that a mesh axis runs over, the one named last changes fastest.
Arguments:
- hidden_in: bfloat16 [4096, 1024], P('dp'), may hold values from -6 to 6
- seq_lengths: int32 [64], P('dp'), may hold values from 0 to 256, as said below
- norm_in: bfloat16 [1024], P('dp'), may hold values from 0.5 to 1.5
- w_z: bfloat16 [1024, 1536], P('dp', 'tensor'), may hold values from -0.1875 to 0.1875
- w_x: bfloat16 [1024, 1536], P('dp', 'tensor'), may hold values from -0.1875 to 0.1875
- w_bc: bfloat16 [1024, 256], P('dp'), may hold values from -0.09375 to 0.09375
- w_dt: bfloat16 [1024, 24], P('dp', 'tensor'), may hold values from -0.1875 to 0.1875
- conv_x: bfloat16 [5, 1536], P(None, 'tensor'), may hold values from -3 to 3
- conv_bc: bfloat16 [5, 256], replicated, may hold values from -3 to 3
- head_params: float32 [3, 24], P(None, 'tensor'), may hold values from -6 to 3
- w_out: bfloat16 [1536, 1024], P('tensor', 'dp'), may hold values from -0.15625 to 0.15625
- w_q: bfloat16 [1024, 512], P('dp', 'tensor'), may hold values from -0.1875 to 0.1875
- key_weight: bfloat16 [1024, 128], P('dp', 'tensor'), may hold values from -0.1875 to 0.1875
- value_weight: bfloat16 [1024, 128], P('dp', 'tensor'), may hold values from -0.1875 to 0.1875
- w_o: bfloat16 [512, 1024], P('tensor', 'dp'), may hold values from -1 to 1
- norm_mlp: bfloat16 [1024], P('dp'), may hold values from 0.5 to 1.5
- w_gate: bfloat16 [1024, 2048], P('dp', 'tensor'), may hold values from -0.1875 to 0.1875
- w_up: bfloat16 [1024, 2048], P('dp', 'tensor'), may hold values from -0.1875 to 0.1875
- w_down: bfloat16 [2048, 1024], P('tensor', 'dp'), may hold values from -0.125 to 0.125
- cotangent: bfloat16 [4096, 1024], P('dp'), may hold values from -6 to 6
Outputs:
- layer_out: float32 [4096, 1024], P('dp')
- grad_in: float32 [4096, 1024], P('dp')
- grad_norm_in: float32 [1024], P('dp')
- grad_w_z: float32 [1024, 1536], P('dp', 'tensor')
- grad_w_x: float32 [1024, 1536], P('dp', 'tensor')
- grad_w_bc: float32 [1024, 256], P('dp')
- grad_w_dt: float32 [1024, 24], P('dp', 'tensor')
- grad_conv_x: float32 [5, 1536], P(None, 'tensor')
- grad_conv_bc: float32 [5, 256], replicated
- grad_head_params: float32 [3, 24], P(None, 'tensor')
- grad_w_out: float32 [1536, 1024], P('tensor', 'dp')
- grad_w_q: float32 [1024, 512], P('dp', 'tensor')
- grad_w_k: float32 [1024, 128], P('dp', 'tensor')
- grad_w_v: float32 [1024, 128], P('dp', 'tensor')
- grad_w_o: float32 [512, 1024], P('tensor', 'dp')
- grad_norm_mlp: float32 [1024], P('dp')
- grad_w_gate: float32 [1024, 2048], P('dp', 'tensor')
- grad_w_up: float32 [1024, 2048], P('dp', 'tensor')
- grad_w_down: float32 [2048, 1024], P('tensor', 'dp')
The draws below stay inside these ranges and needn't reach their ends.
Inputs may be any that keep to these rules, and one draw needn't show every extreme that they name: `seq_lengths`: the 4 lengths of one device sum to at most 256, and to exactly 256 on some device; rows past that sum are padding.
All inputs are finite; a program needn't handle non-finite values.
Results may differ from the reference program's by a relative error of at most 0.012.
Values may be sent and summed in bfloat16 or wider, within the bound.
A program may use at most 128 MiB of HBM per device.

```python
import jax
import jax.numpy as jnp
from jax import lax

MODEL_WIDTH = 1024
HM = 24
NSTATE = 128
CONV = 4
HQ = 8
KEY_VALUE_HEADS = 2
HEAD_WIDTH = 64
FF = 2048
SEQS = 4
TOK_DEV = 256
TOKENS = 4096
DSSM = 1536
N_DP = 16


def draw_seq_lengths(key, part):
    key = jax.random.fold_in(key, 11)
    total_key, full_key, share_key = jax.random.split(key, 3)
    totals = jax.random.randint(total_key, (N_DP,), TOK_DEV // 4, TOK_DEV + 1)
    fullest = jax.random.randint(full_key, (), 0, N_DP)
    device_index = jnp.arange(N_DP)
    shares = jax.random.randint(share_key, (N_DP, SEQS), 1, 8)
    bounds = jnp.cumsum(shares, axis=1) * totals[:, None] // jnp.sum(shares, axis=1, keepdims=True)
    lengths = jnp.diff(jnp.concatenate([jnp.zeros((N_DP, 1), jnp.int32), bounds.astype(jnp.int32)], axis=1), axis=1)
    single = jnp.where(jnp.arange(SEQS) == 0, TOK_DEV, 0)
    lengths = jnp.where((device_index == fullest)[:, None], single[None, :], lengths)
    return lengths.reshape(N_DP * SEQS).astype(jnp.int32)


def draw_head_params(key, part):
    key = jax.random.fold_in(key, 23)
    rate_key, bias_key, skip_key = jax.random.split(key, 3)
    log_rate = jax.random.uniform(rate_key, (HM,), jnp.float32, 0.0, 2.77)
    step_bias = jax.random.uniform(bias_key, (HM,), jnp.float32, -5.0, -2.5)
    skip_gain = jax.random.uniform(skip_key, (HM,), jnp.float32, 0.5, 1.5)
    return jnp.stack([log_rate, step_bias, skip_gain], axis=0)


def block_levels(rng, shape, shards, least, high):
    factor_of = 1.0
    for position, parts in shards:
        draws = jax.random.uniform(jax.random.fold_in(jax.random.fold_in(rng, 6), position), (parts,), jnp.float32, least / len(shards), high / len(shards))
        factor_of = factor_of * jnp.repeat(jnp.exp(draws), shape[position] // parts).reshape((-1,) + (1,) * (len(shape) - 1 - position))
    return factor_of


def gaussian(rng, extent, deviation, most, pieces=(), kind=jnp.bfloat16):
    level = block_levels(rng, extent, pieces, -0.22, 0.18) if pieces else 1.0
    drawn = jax.random.normal(rng, extent, jnp.float32) * deviation * level
    return jnp.minimum(jnp.maximum(drawn, -most), most).astype(kind)


def setup_inputs(seed: int = 0) -> dict:
    splits = jax.random.split(jax.random.key(seed), 21)
    return {
        "hidden_in": gaussian(splits[0], (TOKENS, MODEL_WIDTH), 1.0, 6.0, ((0, 16),)),
        "seq_lengths": draw_seq_lengths(jax.random.fold_in(splits[20], 71), 0),
        "norm_in": jnp.clip(1.0 + 0.1 * jax.random.normal(splits[2], (MODEL_WIDTH,), jnp.float32), 0.5, 1.5).astype(jnp.bfloat16),
        "w_z": gaussian(splits[3], (MODEL_WIDTH, DSSM), MODEL_WIDTH ** -0.5, 0.1875, ((0, 16), (1, 2))),
        "w_x": gaussian(splits[4], (MODEL_WIDTH, DSSM), MODEL_WIDTH ** -0.5, 0.1875, ((0, 16), (1, 2))),
        "w_bc": gaussian(splits[5], (MODEL_WIDTH, 2 * NSTATE), (4 * MODEL_WIDTH) ** -0.5, 0.09375, ((0, 16),)),
        "w_dt": gaussian(splits[6], (MODEL_WIDTH, HM), MODEL_WIDTH ** -0.5, 0.1875, ((0, 16), (1, 2))),
        "conv_x": gaussian(splits[7], (CONV + 1, DSSM), 0.5, 3.0, ((1, 2),)),
        "conv_bc": gaussian(splits[8], (CONV + 1, 2 * NSTATE), 0.5, 3.0),
        "head_params": draw_head_params(jax.random.fold_in(splits[20], 71), 0),
        "w_out": gaussian(splits[10], (DSSM, MODEL_WIDTH), DSSM ** -0.5, 0.15625, ((0, 2), (1, 16))),
        "w_q": gaussian(splits[11], (MODEL_WIDTH, HQ * HEAD_WIDTH), MODEL_WIDTH ** -0.5, 0.1875, ((0, 16), (1, 2))),
        "key_weight": gaussian(splits[12], (MODEL_WIDTH, KEY_VALUE_HEADS * HEAD_WIDTH), MODEL_WIDTH ** -0.5, 0.1875, ((0, 16), (1, 2))),
        "value_weight": gaussian(splits[13], (MODEL_WIDTH, KEY_VALUE_HEADS * HEAD_WIDTH), MODEL_WIDTH ** -0.5, 0.1875, ((0, 16), (1, 2))),
        "w_o": gaussian(splits[14], (HQ * HEAD_WIDTH, MODEL_WIDTH), (HQ * HEAD_WIDTH // 16) ** -0.5, 1.0, ((0, 2), (1, 16))),
        "norm_mlp": jnp.clip(1.0 + 0.1 * jax.random.normal(splits[15], (MODEL_WIDTH,), jnp.float32), 0.5, 1.5).astype(jnp.bfloat16),
        "w_gate": gaussian(splits[16], (MODEL_WIDTH, FF), MODEL_WIDTH ** -0.5, 0.1875, ((0, 16), (1, 2))),
        "w_up": gaussian(splits[17], (MODEL_WIDTH, FF), MODEL_WIDTH ** -0.5, 0.1875, ((0, 16), (1, 2))),
        "w_down": gaussian(splits[18], (FF, MODEL_WIDTH), FF ** -0.5, 0.125, ((0, 2), (1, 16))),
        "cotangent": gaussian(splits[19], (TOKENS, MODEL_WIDTH), 1.0, 6.0, ((0, 16),)),
    }


EPSILON = 1e-05
ROTARY_BASE = 100000000000.0
MASKED = -1e+30
EXACT_PRODUCT = lax.Precision.HIGHEST

@jax.custom_vjp
def reduced_cast(v):
    return lax.optimization_barrier(v.astype(jnp.bfloat16)).astype(jnp.float32)

@jax.custom_vjp
def reduced_cast_backward(v):
    return v

def low_keep(v):
    return (reduced_cast(v), None)

def low_pass(kept, grad):
    return (grad,)

def back_keep(v):
    return (v, None)

def back_low(kept, grad):
    return (reduced_cast(grad),)
reduced_cast.defvjp(low_keep, low_pass)
reduced_cast_backward.defvjp(back_keep, back_low)

def precise_product(left_side, right_side):
    return jnp.dot(left_side, right_side, precision=EXACT_PRODUCT)

def root_norm(values, scale_row):
    return values * lax.rsqrt(lax.optimization_barrier(jnp.mean(values * values, axis=-1, keepdims=True)) + EPSILON) * scale_row

def layout(lengths, count_of_rows):
    row_index = jnp.arange(count_of_rows, dtype=jnp.int32)
    seq_ends = jnp.cumsum(lengths).astype(jnp.int32)
    segment = lax.optimization_barrier(jnp.sum((row_index[:, None] >= seq_ends[None, :]).astype(jnp.int32), axis=1)).astype(jnp.int32)
    slot_index = jnp.arange(lengths.shape[0], dtype=jnp.int32)
    starts = lax.optimization_barrier(jnp.sum(jnp.where(slot_index[None, :] < segment[:, None], lengths[None, :], 0), axis=1)).astype(jnp.int32)
    live_rows = (row_index < seq_ends[-1]).astype(jnp.float32)
    return (segment, row_index - starts, live_rows)

def rotary_embedding(values, token_position, direction):
    half_width = values.shape[-1] // 2
    frequency = ROTARY_BASE ** (-jnp.arange(half_width, dtype=jnp.float32) / half_width)
    angles = token_position.astype(jnp.float32)[:, None] * frequency[None, :]
    cosine = jnp.cos(angles)[:, None, :]
    sine_part = direction * jnp.sin(angles)[:, None, :]
    first_half = values[..., :half_width]
    second_half = values[..., half_width:]
    return jnp.concatenate([first_half * cosine - second_half * sine_part, second_half * cosine + first_half * sine_part], axis=-1)

def causal_conv(values, taps_bias, segment):
    kernel_len = taps_bias.shape[0] - 1
    conv_sum = taps_bias[kernel_len][None, :] + taps_bias[kernel_len - 1][None, :] * values
    for offset in range(1, kernel_len):
        shifted = jnp.concatenate([jnp.zeros((offset, values.shape[1]), values.dtype), values[:-offset]], axis=0)
        earlier = jnp.concatenate([jnp.full((offset,), -1, jnp.int32), segment[:-offset]], axis=0)
        same_doc = (earlier == segment).astype(values.dtype)[:, None]
        conv_sum = conv_sum + taps_bias[kernel_len - 1 - offset][None, :] * shifted * same_doc
    return jax.nn.silu(conv_sum)

def state_mix(mixer_in, bc_act, step_raw, head_params, segment):
    count_of_rows, head_count = step_raw.shape
    state_width = bc_act.shape[1] // 2
    inputs = mixer_in.reshape(count_of_rows, head_count, -1)
    decay_rate = jnp.exp(head_params[0])
    step_size = jax.nn.softplus(step_raw + head_params[1][None, :])
    log_decay = jnp.cumsum(-step_size * decay_rate[None, :], axis=0).T
    row_index = jnp.arange(count_of_rows, dtype=jnp.int32)
    visible = (segment[:, None] == segment[None, :]) & (row_index[None, :] <= row_index[:, None])
    log_gap = log_decay[:, :, None] - log_decay[:, None, :]
    decay_mat = jnp.exp(jnp.where(visible[None], log_gap, -jnp.inf))
    intersection = jnp.dot(bc_act[:, state_width:], bc_act[:, :state_width].T, precision=EXACT_PRODUCT)
    mixing = intersection[None] * decay_mat * step_size.T[:, None, :]
    result = jnp.einsum('hts,shp->thp', mixing, inputs, precision=EXACT_PRODUCT)
    result = result + head_params[2][None, :, None] * inputs
    return result.reshape(count_of_rows, -1)

def attend(queries, key_matrix_rows, value_matrix_rows, segment):
    count_of_rows, head_count, head_size = queries.shape
    kv_count = key_matrix_rows.shape[1]
    grouped = queries.reshape(count_of_rows, kv_count, head_count // kv_count, head_size)
    row_index = jnp.arange(count_of_rows, dtype=jnp.int32)
    visible = (segment[:, None] == segment[None, :]) & (row_index[None, :] <= row_index[:, None])
    scores = reduced_cast_backward(jnp.einsum('tkgd,skd->kgts', grouped, key_matrix_rows, precision=EXACT_PRODUCT))
    logits = jnp.where(visible[None, None], scores * head_size ** (-0.5), MASKED)
    largest = lax.optimization_barrier(jnp.max(logits, axis=-1, keepdims=True))
    weights_exp = jnp.exp(logits - largest)
    attention_weights = weights_exp / lax.optimization_barrier(jnp.sum(weights_exp, axis=-1, keepdims=True))
    attended = jnp.einsum('kgts,skd->tkgd', reduced_cast(attention_weights), value_matrix_rows, precision=EXACT_PRODUCT)
    return attended.reshape(count_of_rows, head_count * head_size)

def layer(params, inputs, lengths):
    norm_in, w_z, w_x, w_bc, w_dt, conv_x, conv_bc, head_params, w_out, w_q, key_weight, value_weight, w_o, norm_mlp, w_gate, w_up, w_down = params
    count_of_rows = inputs.shape[0]
    segment, token_position, live_rows = layout(lengths, count_of_rows)
    live_column = live_rows[:, None]
    normalized_input = reduced_cast(root_norm(inputs, norm_in))
    gate_ssm = reduced_cast_backward(precise_product(normalized_input, w_z))
    conv_in = reduced_cast_backward(precise_product(normalized_input, w_x))
    bc_raw = reduced_cast_backward(precise_product(normalized_input, w_bc))
    step_raw = reduced_cast_backward(precise_product(normalized_input, w_dt))
    bc_act = causal_conv(bc_raw, conv_bc, segment)
    mixed_ssm = state_mix(causal_conv(conv_in, conv_x, segment), bc_act, step_raw, head_params, segment)
    gated_out = reduced_cast(mixed_ssm * jax.nn.silu(gate_ssm))
    queries = reduced_cast(rotary_embedding(reduced_cast_backward(precise_product(normalized_input, w_q)).reshape(count_of_rows, HQ, HEAD_WIDTH), token_position, 1.0))
    key_matrix_rows = reduced_cast(rotary_embedding(reduced_cast_backward(precise_product(normalized_input, key_weight)).reshape(count_of_rows, KEY_VALUE_HEADS, HEAD_WIDTH), token_position, 1.0))
    value_matrix_rows = reduced_cast(reduced_cast_backward(precise_product(normalized_input, value_weight))).reshape(count_of_rows, KEY_VALUE_HEADS, HEAD_WIDTH)
    attended = reduced_cast(reduced_cast_backward(attend(queries, key_matrix_rows, value_matrix_rows, segment)))
    mixed_sum = reduced_cast_backward(precise_product(gated_out, w_out) + precise_product(attended, w_o))
    residual = inputs + live_column * mixed_sum
    normed_mlp = reduced_cast(root_norm(residual, norm_mlp))
    gate_pre = reduced_cast_backward(precise_product(normed_mlp, w_gate))
    up_pre = reduced_cast_backward(precise_product(normed_mlp, w_up))
    activated = reduced_cast(jax.nn.silu(gate_pre) * up_pre)
    return residual + live_column * reduced_cast_backward(precise_product(activated, w_down))

def reference(hidden_in, seq_lengths, norm_in, w_z, w_x, w_bc, w_dt, conv_x, conv_bc, head_params, w_out, w_q, key_weight, value_weight, w_o, norm_mlp, w_gate, w_up, w_down, cotangent):
    params = tuple((array.astype(jnp.float32) for array in (norm_in, w_z, w_x, w_bc, w_dt, conv_x, conv_bc, head_params, w_out, w_q, key_weight, value_weight, w_o, norm_mlp, w_gate, w_up, w_down)))
    blocks = hidden_in.astype(jnp.float32).reshape(N_DP, TOK_DEV, MODEL_WIDTH)
    lengths = seq_lengths.reshape(N_DP, SEQS)
    step_fn = jax.checkpoint(layer)

    def forward(weights, stacked):

        def scan_step(scan_carry, scan_item):
            return (scan_carry, step_fn(weights, scan_item[0], scan_item[1]))
        return lax.scan(scan_step, jnp.zeros((), jnp.float32), (stacked, lengths))[1]
    result, pullback = jax.vjp(forward, params, blocks)
    weight_grads, grad_blocks = pullback(cotangent.astype(jnp.float32).reshape(N_DP, TOK_DEV, MODEL_WIDTH))
    return (result.reshape(TOKENS, MODEL_WIDTH), grad_blocks.reshape(TOKENS, MODEL_WIDTH), weight_grads[0], weight_grads[1], weight_grads[2], weight_grads[3], weight_grads[4], weight_grads[5], weight_grads[6], weight_grads[7], weight_grads[8], weight_grads[9], weight_grads[10], weight_grads[11], weight_grads[12], weight_grads[13], weight_grads[14], weight_grads[15], weight_grads[16])
```

```python
from functools import partial

import jax
import jax.numpy as jnp
from jax import lax
from jax.experimental import pallas as pl
from jax.experimental.pallas import tpu as pltpu
from jax.sharding import PartitionSpec as P

HEAD_WIDTH = 64


EPSILON = 1e-05
ROTARY_BASE = 100000000000.0
MASKED = -1e30
EXACT_PRODUCT = lax.Precision.HIGHEST


def product(left_side, right_side):
    return jnp.dot(left_side, right_side, preferred_element_type=jnp.float32)


def rows_product(left_side, right_side):
    return lax.dot_general(
        left_side, right_side, (((0,), (0,)), ((), ())), preferred_element_type=jnp.float32
    )


def back_product(left_side, right_side):
    return lax.dot_general(
        left_side, right_side, (((1,), (1,)), ((), ())), preferred_element_type=jnp.float32
    )


def root_norm(values, scale_row):
    return (
        values * lax.rsqrt(jnp.mean(values * values, axis=-1, keepdims=True) + EPSILON) * scale_row
    )


def layout(lengths, count_of_rows):
    row_index = jnp.arange(count_of_rows, dtype=jnp.int32)
    seq_ends = jnp.cumsum(lengths)
    segment = jnp.sum((row_index[:, None] >= seq_ends[None, :]).astype(jnp.int32), axis=1)
    slot_index = jnp.arange(lengths.shape[0], dtype=jnp.int32)
    starts = jnp.sum(jnp.where(slot_index[None, :] < segment[:, None], lengths[None, :], 0), axis=1)
    live_rows = (row_index < seq_ends[-1]).astype(jnp.float32)
    return (segment, row_index - starts, live_rows)


def rotary_embedding(values, token_position, direction):
    half_width = values.shape[-1] // 2
    frequency = ROTARY_BASE ** (-jnp.arange(half_width, dtype=jnp.float32) / half_width)
    angles = token_position.astype(jnp.float32)[:, None] * frequency[None, :]
    cosine = jnp.cos(angles)[:, None, :]
    sine_part = direction * jnp.sin(angles)[:, None, :]
    first_half = values[..., :half_width]
    second_half = values[..., half_width:]
    return jnp.concatenate(
        [
            first_half * cosine - second_half * sine_part,
            second_half * cosine + first_half * sine_part,
        ],
        axis=-1,
    )


def causal_conv(values, taps_bias, segment):
    kernel_len = taps_bias.shape[0] - 1
    conv_sum = taps_bias[kernel_len][None, :] + taps_bias[kernel_len - 1][None, :] * values
    for offset in range(1, kernel_len):
        shifted = jnp.concatenate(
            [jnp.zeros((offset, values.shape[1]), values.dtype), values[:-offset]], axis=0
        )
        earlier = jnp.concatenate([jnp.full((offset,), -1, jnp.int32), segment[:-offset]], axis=0)
        same_doc = (earlier == segment).astype(values.dtype)[:, None]
        conv_sum = conv_sum + taps_bias[kernel_len - 1 - offset][None, :] * shifted * same_doc
    return jax.nn.silu(conv_sum)


def state_mix(mixer_in, bc_act, step_raw, head_params, segment):
    count_of_rows, head_count = step_raw.shape
    state_width = bc_act.shape[1] // 2
    inputs = mixer_in.reshape(count_of_rows, head_count, -1)
    decay_rate = jnp.exp(head_params[0])
    step_size = jax.nn.softplus(step_raw + head_params[1][None, :])
    log_decay = jnp.cumsum(-step_size * decay_rate[None, :], axis=0).T
    row_index = jnp.arange(count_of_rows, dtype=jnp.int32)
    visible = (segment[:, None] == segment[None, :]) & (row_index[None, :] <= row_index[:, None])
    log_gap = log_decay[:, :, None] - log_decay[:, None, :]
    decay_mat = jnp.exp(jnp.where(visible[None], log_gap, -jnp.inf))
    intersection = jnp.dot(
        bc_act[:, state_width:], bc_act[:, :state_width].T, precision=EXACT_PRODUCT
    )
    mixing = intersection[None] * decay_mat * step_size.T[:, None, :]
    result = jnp.einsum("hts,shp->thp", mixing, inputs, precision=EXACT_PRODUCT)
    result = result + head_params[2][None, :, None] * inputs
    return result.reshape(count_of_rows, -1)


def mamba_core(gate_ssm, conv_in, step_raw, conv_taps, head_params, bc_act, segment):
    mixer_in = causal_conv(conv_in, conv_taps, segment)
    return state_mix(mixer_in, bc_act, step_raw, head_params, segment) * jax.nn.silu(gate_ssm)


def attend_forward(queries, key_matrix_rows, value_matrix_rows, visible):
    count_of_rows, head_count, head_size = queries.shape
    kv_count = key_matrix_rows.shape[1]
    grouped = queries.reshape(count_of_rows, kv_count, head_count // kv_count, head_size)
    scores = jnp.einsum(
        "tkgd,skd->kgts", grouped, key_matrix_rows, preferred_element_type=jnp.float32
    )
    logits = jnp.where(visible[None, None], scores * head_size ** (-0.5), MASKED)
    largest = jnp.max(logits, axis=-1, keepdims=True)
    weights_exp = jnp.exp(logits - largest)
    totals = jnp.sum(weights_exp, axis=-1, keepdims=True)
    attention_weights = weights_exp / totals
    attended = jnp.einsum(
        "kgts,skd->tkgd",
        attention_weights.astype(jnp.bfloat16),
        value_matrix_rows,
        preferred_element_type=jnp.float32,
    )
    return (attended.reshape(count_of_rows, head_count * head_size), largest + jnp.log(totals))


def attend_backward(queries, key_matrix_rows, value_matrix_rows, visible, log_total, grad_attended):
    count_of_rows, head_count, head_size = queries.shape
    kv_count = key_matrix_rows.shape[1]
    grouped = queries.reshape(count_of_rows, kv_count, head_count // kv_count, head_size)
    grad_grouped = grad_attended.reshape(count_of_rows, kv_count, head_count // kv_count, head_size)
    scores = jnp.einsum(
        "tkgd,skd->kgts", grouped, key_matrix_rows, preferred_element_type=jnp.float32
    )
    logits = jnp.where(visible[None, None], scores * head_size ** (-0.5), MASKED)
    attention_weights = jnp.exp(logits - log_total)
    grad_weights = jnp.einsum(
        "tkgd,skd->kgts", grad_grouped, value_matrix_rows, preferred_element_type=jnp.float32
    )
    inner_sum = jnp.sum(attention_weights * grad_weights, axis=-1, keepdims=True)
    grad_scores = (attention_weights * (grad_weights - inner_sum) * head_size ** (-0.5)).astype(
        jnp.bfloat16
    )
    grad_queries = jnp.einsum(
        "kgts,skd->tkgd", grad_scores, key_matrix_rows, preferred_element_type=jnp.float32
    )
    grad_keys = jnp.einsum(
        "kgts,tkgd->skd", grad_scores, grouped, preferred_element_type=jnp.float32
    )
    grad_values = jnp.einsum(
        "kgts,tkgd->skd",
        attention_weights.astype(jnp.bfloat16),
        grad_grouped,
        preferred_element_type=jnp.float32,
    )
    return (grad_queries.reshape(count_of_rows, head_count, head_size), grad_keys, grad_values)


MESH = pl.DeviceIdType.MESH
VMEM_BYTES = 52 * 1024 * 1024
ADD_ROWS = 16


def place(count):
    me = lax.axis_index("dp")
    core = lax.rem(me, 2)
    column = lax.rem(lax.div(me, 2), 2)
    line = lax.div(me, 4)
    return me, line, column, core, count // 4


def dp_index(line, column, core):
    return (line * 2 + column) * 2 + core


def greet(peers):
    barrier = pltpu.get_barrier_semaphore()
    for peer in peers:
        pl.semaphore_signal(barrier, inc=1, device_id={"dp": peer}, device_id_type=MESH)
    pl.semaphore_wait(barrier, len(peers))


def gather_kernel(count, arrays, *refs):
    shards, wholes = refs[:arrays], refs[arrays : 2 * arrays]
    own_sem, line_send, line_recv, side_send, side_recv, core_send, core_recv = refs[2 * arrays :]
    me, line, column, core, length = place(count)
    side = dp_index(line, 1 - column, core)
    sibling = dp_index(line, column, 1 - core)
    ahead = [dp_index(lax.rem(line + d, length), column, core) for d in range(1, length)]
    greet(ahead + [side, sibling])

    def rows(array, index):
        size = shards[array].shape[0]
        return wholes[array].at[pl.ds(pl.multiple_of(index * size, size), size)]

    def send(source, target, send_sem, recv_sem, peer):
        copy = pltpu.make_async_remote_copy(
            src_ref=source,
            dst_ref=target,
            send_sem=send_sem,
            recv_sem=recv_sem,
            device_id={"dp": peer},
            device_id_type=MESH,
        )
        copy.start()
        return copy

    own, line_copies, side_copies, core_copies = [], {}, {}, {}
    for k in range(arrays):
        mine = rows(k, me)
        side_copies[k, 0] = send(
            shards[k], mine, side_send.at[k, 0], side_recv.at[k, 0], side
        )
        for d in range(1, length):
            line_copies[k, d] = send(
                shards[k], mine, line_send.at[k, d], line_recv.at[k, d], ahead[d - 1]
            )
        core_copies[k, 0] = send(
            shards[k], mine, core_send.at[k, 0], core_recv.at[k, 0], sibling
        )
        copy = pltpu.make_async_copy(shards[k], mine, own_sem.at[k])
        copy.start()
        own.append(copy)

    def pass_side(k):
        for d in range(length):
            side_copies[k, d].wait_recv()
            block = rows(k, dp_index(lax.rem(line - d + length, length), 1 - column, core))
            j = length + d
            core_copies[k, j] = send(
                block, block, core_send.at[k, j], core_recv.at[k, j], sibling
            )

    for k in range(arrays):
        for d in range(1, length):
            line_copies[k, d].wait_recv()
            block = rows(k, dp_index(lax.rem(line - d + length, length), column, core))
            side_copies[k, d] = send(
                block, block, side_send.at[k, d], side_recv.at[k, d], side
            )
            core_copies[k, d] = send(
                block, block, core_send.at[k, d], core_recv.at[k, d], sibling
            )
        if k:
            pass_side(k - 1)
    pass_side(arrays - 1)
    for copy in own:
        copy.wait()
    for copy in core_copies.values():
        copy.wait()
    for copy in list(line_copies.values()) + list(side_copies.values()):
        copy.wait_send()


def gather_rows(shards, count, collective_id):
    if shards[0].shape[0] % 16 or count % 4:
        return tuple(lax.all_gather(shard, "dp", axis=0, tiled=True) for shard in shards)
    arrays, length = len(shards), count // 4
    return pl.pallas_call(
        partial(gather_kernel, count, arrays),
        out_shape=tuple(
            jax.ShapeDtypeStruct((count * s.shape[0], s.shape[1]), s.dtype) for s in shards
        ),
        in_specs=[pl.BlockSpec(memory_space=pl.ANY)] * arrays,
        out_specs=(pl.BlockSpec(memory_space=pl.ANY),) * arrays,
        scratch_shapes=[pltpu.SemaphoreType.DMA((arrays,))]
        + [pltpu.SemaphoreType.DMA((arrays, length))] * 4
        + [pltpu.SemaphoreType.DMA((arrays, 2 * length))] * 2,
        compiler_params=pltpu.CompilerParams(collective_id=collective_id, has_side_effects=True),
    )(*shards)


def scatter_kernel(count, arrays, *refs):
    parts, small = refs[:arrays], refs[arrays]
    sums, small_sum = refs[arrays + 1 : 2 * arrays + 1], refs[2 * arrays + 1]
    rest = refs[2 * arrays + 2 :]
    from_core, from_side, from_line = (
        rest[:arrays],
        rest[arrays : 2 * arrays],
        rest[2 * arrays : 3 * arrays],
    )
    small_core, small_pair, small_side, small_line = rest[3 * arrays : 3 * arrays + 4]
    core_send, core_recv, side_send, side_recv, line_send, line_recv = rest[3 * arrays + 4 :]
    me, line, column, core, length = place(count)
    side = dp_index(line, 1 - column, core)
    sibling = dp_index(line, column, 1 - core)
    ahead = [dp_index(lax.rem(line + d, length), column, core) for d in range(1, length)]
    greet(ahead + [side, sibling])

    def send(source, target, send_sem, recv_sem, peer):
        copy = pltpu.make_async_remote_copy(
            src_ref=source,
            dst_ref=target,
            send_sem=send_sem,
            recv_sem=recv_sem,
            device_id={"dp": peer},
            device_id_type=MESH,
        )
        copy.start()
        return copy

    def part_start(k, d, block_column, block_core):
        size = sums[k].shape[0]
        return pl.multiple_of(
            dp_index(lax.rem(line + d, length), block_column, block_core) * size, size
        )

    def add_into(target, terms, size):
        @pl.loop(0, size // ADD_ROWS)
        def _(step):
            shift = step * ADD_ROWS
            total = None
            for ref, start in terms:
                at = pl.ds(pl.multiple_of(start + shift, ADD_ROWS), ADD_ROWS)
                value = ref[at, :].astype(jnp.float32)
                total = value if total is None else total + value
            ref, start = target
            at = pl.ds(pl.multiple_of(start + shift, ADD_ROWS), ADD_ROWS)
            ref[at, :] = total.astype(ref.dtype)

    core_copies, side_copies, line_copies = {}, {}, {}
    last = arrays
    order = list(range(1, length)) + [0]
    core_copies[last, 0] = send(
        small, small_core, core_send.at[last, 0], core_recv.at[last, 0], sibling
    )
    for other in (1, 0):
        for k in range(arrays):
            size = sums[k].shape[0]
            for d in order:
                j = other * length + d
                block_column = 1 - column if other else column
                start = part_start(k, d, block_column, 1 - core)
                core_copies[k, j] = send(
                    parts[k].at[pl.ds(start, size)],
                    from_core[k].at[pl.ds(j * size, size)],
                    core_send.at[k, j],
                    core_recv.at[k, j],
                    sibling,
                )
    core_copies[last, 0].wait_recv()
    small_pair[...] = small[...] + small_core[...]
    side_copies[last, 0] = send(
        small_pair, small_side, side_send.at[last, 0], side_recv.at[last, 0], side
    )
    for k in range(arrays):
        size = sums[k].shape[0]
        for d in order:
            j = length + d
            core_copies[k, j].wait_recv()
            mine = part_start(k, d, 1 - column, core)
            add_into((from_core[k], j * size), [(from_core[k], j * size), (parts[k], mine)], size)
            side_copies[k, d] = send(
                from_core[k].at[pl.ds(j * size, size)],
                from_side[k].at[pl.ds(d * size, size)],
                side_send.at[k, d],
                side_recv.at[k, d],
                side,
            )
    side_copies[last, 0].wait_recv()
    small_line[line] = small_pair[...] + small_side[...]
    for d in range(1, length):
        line_copies[last, d] = send(
            small_line.at[line],
            small_line.at[line],
            line_send.at[last, d],
            line_recv.at[last, d],
            ahead[d - 1],
        )
    for k in range(arrays):
        size = sums[k].shape[0]
        for d in order:
            core_copies[k, d].wait_recv()
            side_copies[k, d].wait_recv()
            if d:
                mine = part_start(k, d, column, core)
                terms = [
                    (from_side[k], d * size),
                    (from_core[k], d * size),
                    (parts[k], mine),
                ]
                add_into((from_side[k], d * size), terms, size)
                line_copies[k, d] = send(
                    from_side[k].at[pl.ds(d * size, size)],
                    from_line[k].at[pl.ds((d - 1) * size, size)],
                    line_send.at[k, d],
                    line_recv.at[k, d],
                    ahead[d - 1],
                )
    for d in range(1, length):
        line_copies[last, d].wait_recv()
    total = small_line[0]
    for position in range(1, length):
        total = total + small_line[position]
    small_sum[...] = total
    for k in range(arrays):
        size = sums[k].shape[0]
        terms = [
            (from_side[k], 0),
            (from_core[k], 0),
            (parts[k], part_start(k, 0, column, core)),
        ]
        for d in range(1, length):
            line_copies[k, d].wait_recv()
            terms.append((from_line[k], (d - 1) * size))
        add_into((sums[k], 0), terms, size)
    for copies in (core_copies, side_copies, line_copies):
        for copy in copies.values():
            copy.wait_send()


def scatter_rows(parts, small, count, collective_id):
    size = parts[0].shape[0] // count
    if size % 16 or count % 4:
        sums = tuple(
            lax.psum_scatter(
                part.astype(jnp.float32), "dp", scatter_dimension=0, tiled=True
            )
            for part in parts
        )
        return sums + (lax.psum(small, "dp"),)
    arrays, length = len(parts), count // 4
    vmem = pl.BlockSpec(memory_space=pltpu.VMEM)
    widths = [part.shape[1] for part in parts]
    received = [
        pltpu.VMEM((blocks * size, width), jnp.bfloat16)
        for blocks in (2 * length, length, length - 1)
        for width in widths
    ]
    return pl.pallas_call(
        partial(scatter_kernel, count, arrays),
        out_shape=tuple(jax.ShapeDtypeStruct((size, width), jnp.float32) for width in widths)
        + (jax.ShapeDtypeStruct(small.shape, jnp.float32),),
        in_specs=[vmem] * (arrays + 1),
        out_specs=(vmem,) * (arrays + 1),
        scratch_shapes=received
        + [pltpu.VMEM(small.shape, jnp.float32)] * 3
        + [pltpu.VMEM((length,) + small.shape, jnp.float32)]
        + [pltpu.SemaphoreType.DMA((arrays + 1, 2 * length))] * 2
        + [pltpu.SemaphoreType.DMA((arrays + 1, length))] * 4,
        compiler_params=pltpu.CompilerParams(
            collective_id=collective_id, has_side_effects=True, vmem_limit_bytes=VMEM_BYTES
        ),
    )(*parts, small)


def exchange_kernel(arrays, pieces, *refs):
    shares, totals = refs[:arrays], refs[arrays : 2 * arrays]
    mine, theirs = refs[2 * arrays : 3 * arrays], refs[3 * arrays : 4 * arrays]
    send_sem, recv_sem = refs[4 * arrays :]
    peer = 1 - lax.axis_index("tensor")
    barrier = pltpu.get_barrier_semaphore()
    pl.semaphore_signal(barrier, inc=1, device_id={"tensor": peer}, device_id_type=MESH)
    pl.semaphore_wait(barrier, 1)
    copies = {}
    for k in range(arrays):
        size = shares[k].shape[0] // pieces[k]
        for piece in range(pieces[k]):
            at = pl.ds(piece * size, size)
            mine[k][at, :] = shares[k][at, :].astype(jnp.bfloat16)
            copies[k, piece] = pltpu.make_async_remote_copy(
                src_ref=mine[k].at[at],
                dst_ref=theirs[k].at[at],
                send_sem=send_sem.at[k, piece],
                recv_sem=recv_sem.at[k, piece],
                device_id={"tensor": peer},
                device_id_type=MESH,
            )
            copies[k, piece].start()
    for k in range(arrays):
        size = shares[k].shape[0] // pieces[k]
        for piece in range(pieces[k]):
            at = pl.ds(piece * size, size)
            copies[k, piece].wait()
            totals[k][at, :] = mine[k][at, :].astype(jnp.float32) + theirs[k][at, :].astype(
                jnp.float32
            )


def tensor_sum(shares, ways, collective_id):
    if ways != 2:
        return tuple(lax.psum(share, "tensor") for share in shares)
    arrays = len(shares)
    pieces = tuple(4 if share.shape[0] % 64 == 0 else 1 for share in shares)
    vmem = pl.BlockSpec(memory_space=pltpu.VMEM)
    buffers = [pltpu.VMEM(share.shape, jnp.bfloat16) for share in shares]
    return pl.pallas_call(
        partial(exchange_kernel, arrays, pieces),
        out_shape=tuple(jax.ShapeDtypeStruct(share.shape, jnp.float32) for share in shares),
        in_specs=[vmem] * arrays,
        out_specs=(vmem,) * arrays,
        scratch_shapes=buffers + buffers + [pltpu.SemaphoreType.DMA((arrays, 4))] * 2,
        compiler_params=pltpu.CompilerParams(
            collective_id=collective_id, has_side_effects=True, vmem_limit_bytes=VMEM_BYTES
        ),
    )(*shares)


def body(
    hidden_in,
    seq_lengths,
    norm_in,
    w_z,
    w_x,
    w_bc,
    w_dt,
    conv_x,
    conv_bc,
    head_params,
    w_out,
    w_q,
    key_weight,
    value_weight,
    w_o,
    norm_mlp,
    w_gate,
    w_up,
    w_down,
    cotangent,
):
    count = lax.axis_size("dp")
    ways = lax.axis_size("tensor")
    width_z, width_bc, width_dt = w_z.shape[1], w_bc.shape[1], w_dt.shape[1]
    width_q, width_k, width_o = w_q.shape[1], key_weight.shape[1], w_o.shape[0]
    width_ff = w_gate.shape[1]
    thin = jnp.concatenate([w_dt, norm_in[:, None], norm_mlp[:, None]], axis=1)
    thin = jnp.pad(thin, ((0, 0), (0, -thin.shape[1] % 128)))
    packed_in, packed_out, full_glu, down_t = gather_rows(
        (
            jnp.concatenate([w_z, w_x, w_bc, w_q, key_weight, value_weight, thin], axis=1),
            jnp.concatenate([w_out.T, w_o.T], axis=1),
            jnp.concatenate([w_gate, w_up], axis=1),
            w_down.T,
        ),
        count,
        0,
    )
    edges = [0]
    for width in (width_z, width_z, width_bc, width_q, width_k, width_k, width_dt):
        edges.append(edges[-1] + width)
    gain_in = packed_in[:, edges[7]]
    gain_mlp = packed_in[:, edges[7] + 1]
    full_in = packed_in[:, : edges[7]]
    inputs = hidden_in.astype(jnp.float32)
    count_of_rows = inputs.shape[0]
    segment, token_position, live_rows = layout(seq_lengths, count_of_rows)
    live_column = live_rows[:, None]
    row_index = jnp.arange(count_of_rows, dtype=jnp.int32)
    visible = (segment[:, None] == segment[None, :]) & (row_index[None, :] <= row_index[:, None])
    normed_full, norm_in_pull = jax.vjp(root_norm, inputs, gain_in.astype(jnp.float32))
    normalized_input = normed_full.astype(jnp.bfloat16)
    projected = product(normalized_input, full_in)
    gate_ssm, conv_in, bc_raw, q_raw, k_raw, v_raw, step_raw = (
        projected[:, left:right] for left, right in zip(edges[:-1], edges[1:])
    )
    bc_act, bc_pull = jax.vjp(
        partial(causal_conv, segment=segment), bc_raw, conv_bc.astype(jnp.float32)
    )
    gated_full, mamba_pull = jax.vjp(
        partial(mamba_core, segment=segment),
        gate_ssm,
        conv_in,
        step_raw,
        conv_x.astype(jnp.float32),
        head_params,
        bc_act,
    )
    gated_out = gated_full.astype(jnp.bfloat16)
    query_heads = width_q // HEAD_WIDTH
    kv_heads = width_k // HEAD_WIDTH
    queries = rotary_embedding(
        q_raw.reshape(count_of_rows, query_heads, HEAD_WIDTH),
        token_position,
        1.0,
    ).astype(jnp.bfloat16)
    key_matrix_rows = rotary_embedding(
        k_raw.reshape(count_of_rows, kv_heads, HEAD_WIDTH),
        token_position,
        1.0,
    ).astype(jnp.bfloat16)
    value_matrix_rows = (
        v_raw.astype(jnp.bfloat16)
        .reshape(count_of_rows, kv_heads, HEAD_WIDTH)
    )
    attended_full, log_total = attend_forward(queries, key_matrix_rows, value_matrix_rows, visible)
    attended = attended_full.astype(jnp.bfloat16)
    mixed_in = jnp.concatenate([gated_out, attended], axis=1)
    (mixed_sum,) = tensor_sum((back_product(mixed_in, packed_out),), ways, 1)
    residual = inputs + live_column * mixed_sum
    normed_mlp_full, norm_mlp_pull = jax.vjp(root_norm, residual, gain_mlp.astype(jnp.float32))
    normed_mlp = normed_mlp_full.astype(jnp.bfloat16)
    glu_pre = product(normed_mlp, full_glu)
    gate_pre, up_pre = glu_pre[:, :width_ff], glu_pre[:, width_ff:]
    activated = (jax.nn.silu(gate_pre) * up_pre).astype(jnp.bfloat16)
    (mlp_out,) = tensor_sum((back_product(activated, down_t),), ways, 2)
    layer_out = residual + live_column * mlp_out
    grad_out = cotangent.astype(jnp.float32)
    grad_mlp = (live_column * grad_out).astype(jnp.bfloat16)
    grad_act = product(grad_mlp, down_t)
    sigmoid_gate = jax.nn.sigmoid(gate_pre)
    grad_gate = (grad_act * up_pre * sigmoid_gate * (1.0 + gate_pre * (1.0 - sigmoid_gate))).astype(
        jnp.bfloat16
    )
    grad_up = (grad_act * jax.nn.silu(gate_pre)).astype(jnp.bfloat16)
    grad_glu = jnp.concatenate([grad_gate, grad_up], axis=1)
    part_down = rows_product(grad_mlp, activated).astype(jnp.bfloat16)
    part_glu = rows_product(normed_mlp, grad_glu).astype(jnp.bfloat16)
    (grad_normed_mlp,) = tensor_sum((back_product(grad_glu, full_glu),), ways, 3)
    grad_residual_norm, part_gain_mlp = norm_mlp_pull(grad_normed_mlp)
    grad_residual = grad_out + grad_residual_norm
    grad_mixed = (live_column * grad_residual).astype(jnp.bfloat16)
    grad_mixed_in = product(grad_mixed, packed_out)
    grad_gated = grad_mixed_in[:, :width_z]
    grad_attended = grad_mixed_in[:, width_z:].astype(jnp.bfloat16)
    part_out = rows_product(grad_mixed, mixed_in).astype(jnp.bfloat16)
    grad_queries, grad_keys, grad_values = attend_backward(
        queries, key_matrix_rows, value_matrix_rows, visible, log_total, grad_attended
    )
    grad_q = (
        rotary_embedding(grad_queries, token_position, -1.0)
        .reshape(count_of_rows, -1)
        .astype(jnp.bfloat16)
    )
    grad_k = (
        rotary_embedding(grad_keys, token_position, -1.0)
        .reshape(count_of_rows, -1)
        .astype(jnp.bfloat16)
    )
    grad_v = grad_values.reshape(count_of_rows, -1).astype(jnp.bfloat16)
    grad_gate_ssm, grad_conv_in, grad_step, part_conv_x, part_heads, bc_share = mamba_pull(
        grad_gated
    )
    bc_raw_share, conv_bc_share = bc_pull(bc_share)
    grad_gate_ssm = grad_gate_ssm.astype(jnp.bfloat16)
    grad_conv_in = grad_conv_in.astype(jnp.bfloat16)
    grad_step = grad_step.astype(jnp.bfloat16)
    grad_projected = jnp.concatenate(
        [
            grad_gate_ssm,
            grad_conv_in,
            bc_raw_share.astype(jnp.bfloat16),
            grad_q,
            grad_k,
            grad_v,
            grad_step,
        ],
        axis=1,
    )
    conv_rows = conv_bc.shape[0]
    bc_terms = jnp.concatenate(
        [bc_raw_share, jnp.pad(conv_bc_share, ((0, -conv_rows % 16), (0, 0)))], axis=0
    )
    grad_normed, bc_sums = tensor_sum(
        (back_product(grad_projected, full_in), bc_terms), ways, 4
    )
    grad_bc_raw = bc_sums[:count_of_rows].astype(jnp.bfloat16)
    part_conv_bc = bc_sums[count_of_rows : count_of_rows + conv_rows]
    grad_input_norm, part_gain_in = norm_in_pull(grad_normed)
    grad_in = grad_residual + grad_input_norm
    grad_projected = jnp.concatenate(
        [
            grad_gate_ssm,
            grad_conv_in,
            grad_bc_raw,
            grad_q,
            grad_k,
            grad_v,
            grad_step,
        ],
        axis=1,
    )
    part_in = jnp.concatenate(
        [
            rows_product(normalized_input, grad_projected),
            part_gain_in[:, None],
            part_gain_mlp[:, None],
        ],
        axis=1,
    ).astype(jnp.bfloat16)
    part_in = jnp.pad(part_in, ((0, 0), (0, packed_in.shape[1] - part_in.shape[1])))
    head_rows, head_count = head_params.shape
    small = jnp.concatenate(
        [
            jnp.pad(part_conv_x, ((0, 8 - conv_rows), (0, 0))),
            jnp.pad(part_conv_bc, ((0, 8 - conv_rows), (0, 0))),
            jnp.pad(part_heads, ((0, 8 - head_rows), (0, -head_count % 128))),
        ],
        axis=1,
    )
    sum_in, sum_out_o, sum_glu, sum_down, sum_small = scatter_rows(
        (part_in, part_out, part_glu, part_down), small, count, 5
    )
    sum_z, sum_x, sum_bc, sum_q, sum_k, sum_v, sum_dt = (
        sum_in[:, left:right] for left, right in zip(edges[:-1], edges[1:])
    )
    sum_gain_in = sum_in[:, edges[7]]
    sum_gain_mlp = sum_in[:, edges[7] + 1]
    sum_out = sum_out_o[:, :width_z].T
    sum_o = sum_out_o[:, width_z:].T
    sum_gate, sum_up = sum_glu[:, :width_ff], sum_glu[:, width_ff:]
    sum_down = sum_down.T
    sum_conv_x = sum_small[:conv_rows, :width_z]
    sum_conv_bc = sum_small[:conv_rows, width_z : width_z + width_bc]
    sum_heads = sum_small[:head_rows, width_z + width_bc : width_z + width_bc + head_count]
    return (
        layer_out,
        grad_in,
        sum_gain_in,
        sum_z,
        sum_x,
        sum_bc,
        sum_dt,
        sum_conv_x,
        sum_conv_bc,
        sum_heads,
        sum_out,
        sum_q,
        sum_k,
        sum_v,
        sum_o,
        sum_gain_mlp,
        sum_gate,
        sum_up,
        sum_down,
    )


def solution(mesh):
    return jax.shard_map(
        body,
        mesh=mesh,
        in_specs=(
            P("dp", None),
            P("dp"),
            P("dp"),
            P("dp", "tensor"),
            P("dp", "tensor"),
            P("dp", None),
            P("dp", "tensor"),
            P(None, "tensor"),
            P(),
            P(None, "tensor"),
            P("tensor", "dp"),
            P("dp", "tensor"),
            P("dp", "tensor"),
            P("dp", "tensor"),
            P("tensor", "dp"),
            P("dp"),
            P("dp", "tensor"),
            P("dp", "tensor"),
            P("tensor", "dp"),
            P("dp", None),
        ),
        out_specs=(
            P("dp", None),
            P("dp", None),
            P("dp"),
            P("dp", "tensor"),
            P("dp", "tensor"),
            P("dp", None),
            P("dp", "tensor"),
            P(None, "tensor"),
            P(),
            P(None, "tensor"),
            P("tensor", "dp"),
            P("dp", "tensor"),
            P("dp", "tensor"),
            P("dp", "tensor"),
            P("tensor", "dp"),
            P("dp"),
            P("dp", "tensor"),
            P("dp", "tensor"),
            P("tensor", "dp"),
        ),
        check_vma=False,
    )
```

```python
from functools import partial

import jax
import jax.numpy as jnp
from jax import lax
from jax.experimental import pallas as pl
from jax.experimental.pallas import tpu as pltpu
from jax.sharding import PartitionSpec as P

HEAD_WIDTH = 64


EPSILON = 1e-05
ROTARY_BASE = 100000000000.0
MASKED = -1e30
EXACT_PRODUCT = lax.Precision.HIGHEST


def product(left_side, right_side):
    return jnp.dot(left_side, right_side, preferred_element_type=jnp.float32)


def rows_product(left_side, right_side):
    return lax.dot_general(
        left_side, right_side, (((0,), (0,)), ((), ())), preferred_element_type=jnp.float32
    )


def back_product(left_side, right_side):
    return lax.dot_general(
        left_side, right_side, (((1,), (1,)), ((), ())), preferred_element_type=jnp.float32
    )


def root_norm(values, scale_row):
    return (
        values * lax.rsqrt(jnp.mean(values * values, axis=-1, keepdims=True) + EPSILON) * scale_row
    )


def layout(lengths, count_of_rows):
    row_index = jnp.arange(count_of_rows, dtype=jnp.int32)
    seq_ends = jnp.cumsum(lengths)
    segment = jnp.sum((row_index[:, None] >= seq_ends[None, :]).astype(jnp.int32), axis=1)
    slot_index = jnp.arange(lengths.shape[0], dtype=jnp.int32)
    starts = jnp.sum(jnp.where(slot_index[None, :] < segment[:, None], lengths[None, :], 0), axis=1)
    live_rows = (row_index < seq_ends[-1]).astype(jnp.float32)
    return (segment, row_index - starts, live_rows)


def rotary_embedding(values, token_position, direction):
    half_width = values.shape[-1] // 2
    frequency = ROTARY_BASE ** (-jnp.arange(half_width, dtype=jnp.float32) / half_width)
    angles = token_position.astype(jnp.float32)[:, None] * frequency[None, :]
    cosine = jnp.cos(angles)[:, None, :]
    sine_part = direction * jnp.sin(angles)[:, None, :]
    first_half = values[..., :half_width]
    second_half = values[..., half_width:]
    return jnp.concatenate(
        [
            first_half * cosine - second_half * sine_part,
            second_half * cosine + first_half * sine_part,
        ],
        axis=-1,
    )


def causal_conv(values, taps_bias, segment):
    kernel_len = taps_bias.shape[0] - 1
    conv_sum = taps_bias[kernel_len][None, :] + taps_bias[kernel_len - 1][None, :] * values
    for offset in range(1, kernel_len):
        shifted = jnp.concatenate(
            [jnp.zeros((offset, values.shape[1]), values.dtype), values[:-offset]], axis=0
        )
        earlier = jnp.concatenate([jnp.full((offset,), -1, jnp.int32), segment[:-offset]], axis=0)
        same_doc = (earlier == segment).astype(values.dtype)[:, None]
        conv_sum = conv_sum + taps_bias[kernel_len - 1 - offset][None, :] * shifted * same_doc
    return jax.nn.silu(conv_sum)


def state_mix(mixer_in, bc_act, step_raw, head_params, segment):
    count_of_rows, head_count = step_raw.shape
    state_width = bc_act.shape[1] // 2
    inputs = mixer_in.reshape(count_of_rows, head_count, -1)
    decay_rate = jnp.exp(head_params[0])
    step_size = jax.nn.softplus(step_raw + head_params[1][None, :])
    log_decay = jnp.cumsum(-step_size * decay_rate[None, :], axis=0).T
    row_index = jnp.arange(count_of_rows, dtype=jnp.int32)
    visible = (segment[:, None] == segment[None, :]) & (row_index[None, :] <= row_index[:, None])
    log_gap = log_decay[:, :, None] - log_decay[:, None, :]
    decay_mat = jnp.exp(jnp.where(visible[None], log_gap, -jnp.inf))
    intersection = jnp.dot(
        bc_act[:, state_width:], bc_act[:, :state_width].T, precision=EXACT_PRODUCT
    )
    mixing = intersection[None] * decay_mat * step_size.T[:, None, :]
    result = jnp.einsum("hts,shp->thp", mixing, inputs, precision=EXACT_PRODUCT)
    result = result + head_params[2][None, :, None] * inputs
    return result.reshape(count_of_rows, -1)


def mamba_core(gate_ssm, conv_in, step_raw, conv_taps, head_params, bc_act, segment):
    mixer_in = causal_conv(conv_in, conv_taps, segment)
    return state_mix(mixer_in, bc_act, step_raw, head_params, segment) * jax.nn.silu(gate_ssm)


def attend_forward(queries, key_matrix_rows, value_matrix_rows, visible):
    count_of_rows, head_count, head_size = queries.shape
    kv_count = key_matrix_rows.shape[1]
    grouped = queries.reshape(count_of_rows, kv_count, head_count // kv_count, head_size)
    scores = jnp.einsum(
        "tkgd,skd->kgts", grouped, key_matrix_rows, preferred_element_type=jnp.float32
    )
    logits = jnp.where(visible[None, None], scores * head_size ** (-0.5), MASKED)
    largest = jnp.max(logits, axis=-1, keepdims=True)
    weights_exp = jnp.exp(logits - largest)
    totals = jnp.sum(weights_exp, axis=-1, keepdims=True)
    attention_weights = weights_exp / totals
    attended = jnp.einsum(
        "kgts,skd->tkgd",
        attention_weights.astype(jnp.bfloat16),
        value_matrix_rows,
        preferred_element_type=jnp.float32,
    )
    return (attended.reshape(count_of_rows, head_count * head_size), largest + jnp.log(totals))


def attend_backward(queries, key_matrix_rows, value_matrix_rows, visible, log_total, grad_attended):
    count_of_rows, head_count, head_size = queries.shape
    kv_count = key_matrix_rows.shape[1]
    grouped = queries.reshape(count_of_rows, kv_count, head_count // kv_count, head_size)
    grad_grouped = grad_attended.reshape(count_of_rows, kv_count, head_count // kv_count, head_size)
    scores = jnp.einsum(
        "tkgd,skd->kgts", grouped, key_matrix_rows, preferred_element_type=jnp.float32
    )
    logits = jnp.where(visible[None, None], scores * head_size ** (-0.5), MASKED)
    attention_weights = jnp.exp(logits - log_total)
    grad_weights = jnp.einsum(
        "tkgd,skd->kgts", grad_grouped, value_matrix_rows, preferred_element_type=jnp.float32
    )
    inner_sum = jnp.sum(attention_weights * grad_weights, axis=-1, keepdims=True)
    grad_scores = (attention_weights * (grad_weights - inner_sum) * head_size ** (-0.5)).astype(
        jnp.bfloat16
    )
    grad_queries = jnp.einsum(
        "kgts,skd->tkgd", grad_scores, key_matrix_rows, preferred_element_type=jnp.float32
    )
    grad_keys = jnp.einsum(
        "kgts,tkgd->skd", grad_scores, grouped, preferred_element_type=jnp.float32
    )
    grad_values = jnp.einsum(
        "kgts,tkgd->skd",
        attention_weights.astype(jnp.bfloat16),
        grad_grouped,
        preferred_element_type=jnp.float32,
    )
    return (grad_queries.reshape(count_of_rows, head_count, head_size), grad_keys, grad_values)


MESH = pl.DeviceIdType.MESH
VMEM_BYTES = 52 * 1024 * 1024
ADD_ROWS = 16


def place(count):
    me = lax.axis_index("dp")
    core = lax.rem(me, 2)
    column = lax.rem(lax.div(me, 2), 2)
    line = lax.div(me, 4)
    return me, line, column, core, count // 4


def dp_index(line, column, core):
    return (line * 2 + column) * 2 + core


def greet(peers, partner=None):
    barrier = pltpu.get_barrier_semaphore()
    if partner is not None:
        pl.semaphore_signal(barrier, inc=1, device_id={"tensor": partner}, device_id_type=MESH)
    for peer in peers:
        pl.semaphore_signal(barrier, inc=1, device_id={"dp": peer}, device_id_type=MESH)
    pl.semaphore_wait(barrier, len(peers) + (partner is not None))


def gather_kernel(count, arrays, *refs):
    shards, wholes = refs[:arrays], refs[arrays : 2 * arrays]
    own_sem, line_send, line_recv, side_send, side_recv, core_send, core_recv = refs[2 * arrays :]
    me, line, column, core, length = place(count)
    side = dp_index(line, 1 - column, core)
    sibling = dp_index(line, column, 1 - core)
    ahead = [dp_index(lax.rem(line + d, length), column, core) for d in range(1, length)]
    greet(ahead + [side, sibling])

    def rows(array, index):
        size = shards[array].shape[0]
        return wholes[array].at[pl.ds(pl.multiple_of(index * size, size), size)]

    def send(source, target, send_sem, recv_sem, peer):
        copy = pltpu.make_async_remote_copy(
            src_ref=source,
            dst_ref=target,
            send_sem=send_sem,
            recv_sem=recv_sem,
            device_id={"dp": peer},
            device_id_type=MESH,
        )
        copy.start()
        return copy

    own, line_copies, side_copies, core_copies = [], {}, {}, {}
    for k in range(arrays):
        mine = rows(k, me)
        side_copies[k, 0] = send(
            shards[k], mine, side_send.at[k, 0], side_recv.at[k, 0], side
        )
        for d in range(1, length):
            line_copies[k, d] = send(
                shards[k], mine, line_send.at[k, d], line_recv.at[k, d], ahead[d - 1]
            )
        core_copies[k, 0] = send(
            shards[k], mine, core_send.at[k, 0], core_recv.at[k, 0], sibling
        )
        copy = pltpu.make_async_copy(shards[k], mine, own_sem.at[k])
        copy.start()
        own.append(copy)

    def pass_side(k):
        for d in range(length):
            side_copies[k, d].wait_recv()
            block = rows(k, dp_index(lax.rem(line - d + length, length), 1 - column, core))
            j = length + d
            core_copies[k, j] = send(
                block, block, core_send.at[k, j], core_recv.at[k, j], sibling
            )

    for k in range(arrays):
        for d in range(1, length):
            line_copies[k, d].wait_recv()
            block = rows(k, dp_index(lax.rem(line - d + length, length), column, core))
            side_copies[k, d] = send(
                block, block, side_send.at[k, d], side_recv.at[k, d], side
            )
            core_copies[k, d] = send(
                block, block, core_send.at[k, d], core_recv.at[k, d], sibling
            )
        if k:
            pass_side(k - 1)
    pass_side(arrays - 1)
    for copy in own:
        copy.wait()
    for copy in core_copies.values():
        copy.wait()
    for copy in list(line_copies.values()) + list(side_copies.values()):
        copy.wait_send()


def gather_rows(shards, count, collective_id):
    if shards[0].shape[0] % 16 or count % 4:
        return tuple(lax.all_gather(shard, "dp", axis=0, tiled=True) for shard in shards)
    arrays, length = len(shards), count // 4
    return pl.pallas_call(
        partial(gather_kernel, count, arrays),
        out_shape=tuple(
            jax.ShapeDtypeStruct((count * s.shape[0], s.shape[1]), s.dtype) for s in shards
        ),
        in_specs=[pl.BlockSpec(memory_space=pl.ANY)] * arrays,
        out_specs=(pl.BlockSpec(memory_space=pl.ANY),) * arrays,
        scratch_shapes=[pltpu.SemaphoreType.DMA((arrays,))]
        + [pltpu.SemaphoreType.DMA((arrays, length))] * 4
        + [pltpu.SemaphoreType.DMA((arrays, 2 * length))] * 2,
        compiler_params=pltpu.CompilerParams(collective_id=collective_id, has_side_effects=True),
    )(*shards)


def scatter_kernel(count, arrays, pairs, paired, paired_small, *refs):
    parts, small = refs[:arrays], refs[arrays]
    shares, refs = refs[arrays + 1 : arrays + 1 + pairs], refs[arrays + 1 + pairs :]
    sums, small_sum = refs[:arrays], refs[arrays]
    totals, rest = refs[arrays + 1 : arrays + 1 + pairs], refs[arrays + 1 + pairs :]
    theirs, rest = rest[:pairs], rest[pairs:]
    pair_in, pair_small, pair_send, pair_recv = rest[:4]
    rest = rest[4:]
    partner = 1 - lax.axis_index("tensor")
    from_core, from_side, from_line = (
        rest[:arrays],
        rest[arrays : 2 * arrays],
        rest[2 * arrays : 3 * arrays],
    )
    small_core, small_pair, small_side, small_line = rest[3 * arrays : 3 * arrays + 4]
    core_send, core_recv, side_send, side_recv, line_send, line_recv = rest[3 * arrays + 4 :]
    me, line, column, core, length = place(count)
    side = dp_index(line, 1 - column, core)
    sibling = dp_index(line, column, 1 - core)
    ahead = [dp_index(lax.rem(line + d, length), column, core) for d in range(1, length)]
    greet(ahead + [side, sibling], partner)

    def swap(source, target, index):
        copy = pltpu.make_async_remote_copy(
            src_ref=source,
            dst_ref=target,
            send_sem=pair_send.at[index],
            recv_sem=pair_recv.at[index],
            device_id={"tensor": partner},
            device_id_type=MESH,
        )
        copy.start()
        return copy

    def send(source, target, send_sem, recv_sem, peer):
        copy = pltpu.make_async_remote_copy(
            src_ref=source,
            dst_ref=target,
            send_sem=send_sem,
            recv_sem=recv_sem,
            device_id={"dp": peer},
            device_id_type=MESH,
        )
        copy.start()
        return copy

    def part_start(k, d, block_column, block_core):
        size = sums[k].shape[0]
        return pl.multiple_of(
            dp_index(lax.rem(line + d, length), block_column, block_core) * size, size
        )

    def add_into(target, terms, size):
        @pl.loop(0, size // ADD_ROWS)
        def _(step):
            shift = step * ADD_ROWS
            total = None
            for ref, start in terms:
                at = pl.ds(pl.multiple_of(start + shift, ADD_ROWS), ADD_ROWS)
                value = ref[at, :].astype(jnp.float32)
                total = value if total is None else total + value
            ref, start = target
            at = pl.ds(pl.multiple_of(start + shift, ADD_ROWS), ADD_ROWS)
            ref[at, :] = total.astype(ref.dtype)

    core_copies, side_copies, line_copies = {}, {}, {}
    last = arrays
    core_copies[last, 0] = send(
        small, small_core, core_send.at[last, 0], core_recv.at[last, 0], sibling
    )
    far_first = [(k, d) for k in range(arrays) for d in range(1, length)]
    far_first += [(k, 0) for k in range(arrays)]
    for other in (1, 0):
        for k, d in far_first:
            size = sums[k].shape[0]
            j = other * length + d
            block_column = 1 - column if other else column
            start = part_start(k, d, block_column, 1 - core)
            core_copies[k, j] = send(
                parts[k].at[pl.ds(start, size)],
                from_core[k].at[pl.ds(j * size, size)],
                core_send.at[k, j],
                core_recv.at[k, j],
                sibling,
            )
    pair_copies = [swap(shares[i], theirs[i], i) for i in range(pairs)]
    core_copies[last, 0].wait_recv()
    small_pair[...] = small[...] + small_core[...]
    side_copies[last, 0] = send(
        small_pair, small_side, side_send.at[last, 0], side_recv.at[last, 0], side
    )
    for k, d in far_first:
        size = sums[k].shape[0]
        j = length + d
        core_copies[k, j].wait_recv()
        mine = part_start(k, d, 1 - column, core)
        add_into((from_core[k], j * size), [(from_core[k], j * size), (parts[k], mine)], size)
        side_copies[k, d] = send(
            from_core[k].at[pl.ds(j * size, size)],
            from_side[k].at[pl.ds(d * size, size)],
            side_send.at[k, d],
            side_recv.at[k, d],
            side,
        )
    side_copies[last, 0].wait_recv()
    small_line[line] = small_pair[...] + small_side[...]
    for d in range(1, length):
        line_copies[last, d] = send(
            small_line.at[line],
            small_line.at[line],
            line_send.at[last, d],
            line_recv.at[last, d],
            ahead[d - 1],
        )
    for k, d in far_first:
        size = sums[k].shape[0]
        core_copies[k, d].wait_recv()
        side_copies[k, d].wait_recv()
        if d:
            mine = part_start(k, d, column, core)
            terms = [
                (from_side[k], d * size),
                (from_core[k], d * size),
                (parts[k], mine),
            ]
            add_into((from_side[k], d * size), terms, size)
            line_copies[k, d] = send(
                from_side[k].at[pl.ds(d * size, size)],
                from_line[k].at[pl.ds((d - 1) * size, size)],
                line_send.at[k, d],
                line_recv.at[k, d],
                ahead[d - 1],
            )
    for i in range(pairs):
        pair_copies[i].wait()

        @pl.loop(0, shares[i].shape[0] // ADD_ROWS)
        def _(step):
            at = pl.ds(pl.multiple_of(step * ADD_ROWS, ADD_ROWS), ADD_ROWS)
            totals[i][at, :] = shares[i][at, :].astype(jnp.float32) + theirs[i][at, :].astype(
                jnp.float32
            )

    for d in range(1, length):
        line_copies[last, d].wait_recv()
    total = small_line[0]
    for position in range(1, length):
        total = total + small_line[position]
    small_sum[...] = total
    small_pairs = small_sum.at[:, pl.ds(0, paired_small)]
    swap_small = swap(small_pairs, pair_small, pairs)
    for k in range(arrays):
        size = sums[k].shape[0]
        terms = [
            (from_side[k], 0),
            (from_core[k], 0),
            (parts[k], part_start(k, 0, column, core)),
        ]
        for d in range(1, length):
            line_copies[k, d].wait_recv()
            terms.append((from_line[k], (d - 1) * size))
        add_into((sums[k], 0), terms, size)
        if k == 0:
            in_pairs = sums[0].at[:, pl.ds(paired[0], paired[1])]
            swap_in = swap(in_pairs, pair_in, pairs + 1)
    swap_small.wait()
    small_pairs[...] = small_pairs[...] + pair_small[...]
    swap_in.wait()
    in_pairs[...] = in_pairs[...] + pair_in[...]
    for copies in (core_copies, side_copies, line_copies):
        for copy in copies.values():
            copy.wait_send()


def scatter_rows(parts, small, shares, paired, paired_small, count, ways, collective_id):
    size = parts[0].shape[0] // count
    if size % 16 or count % 4 or ways != 2:
        sums = [
            lax.psum_scatter(part.astype(jnp.float32), "dp", scatter_dimension=0, tiled=True)
            for part in parts
        ]
        left, right = paired[0], paired[0] + paired[1]
        middle = lax.psum(sums[0][:, left:right], "tensor")
        sums[0] = jnp.concatenate([sums[0][:, :left], middle, sums[0][:, right:]], axis=1)
        small = lax.psum(small, "dp")
        both = lax.psum(small[:, :paired_small], "tensor")
        small = jnp.concatenate([both, small[:, paired_small:]], axis=1)
        totals = [lax.psum(share, "tensor").astype(jnp.float32) for share in shares]
        return (*sums, small, *totals)
    arrays, pairs, length = len(parts), len(shares), count // 4
    vmem = pl.BlockSpec(memory_space=pltpu.VMEM)
    widths = [part.shape[1] for part in parts]
    received = [
        pltpu.VMEM((blocks * size, width), jnp.bfloat16)
        for blocks in (2 * length, length, length - 1)
        for width in widths
    ]
    return pl.pallas_call(
        partial(scatter_kernel, count, arrays, pairs, paired, paired_small),
        out_shape=tuple(jax.ShapeDtypeStruct((size, width), jnp.float32) for width in widths)
        + (jax.ShapeDtypeStruct(small.shape, jnp.float32),)
        + tuple(jax.ShapeDtypeStruct(share.shape, jnp.float32) for share in shares),
        in_specs=[vmem] * (arrays + 1 + pairs),
        out_specs=(vmem,) * (arrays + 1 + pairs),
        scratch_shapes=[pltpu.VMEM(share.shape, share.dtype) for share in shares]
        + [
            pltpu.VMEM((size, paired[1]), jnp.float32),
            pltpu.VMEM((small.shape[0], paired_small), jnp.float32),
        ]
        + [pltpu.SemaphoreType.DMA((pairs + 2,))] * 2
        + received
        + [pltpu.VMEM(small.shape, jnp.float32)] * 3
        + [pltpu.VMEM((length,) + small.shape, jnp.float32)]
        + [pltpu.SemaphoreType.DMA((arrays + 1, 2 * length))] * 2
        + [pltpu.SemaphoreType.DMA((arrays + 1, length))] * 4,
        compiler_params=pltpu.CompilerParams(
            collective_id=collective_id, has_side_effects=True, vmem_limit_bytes=VMEM_BYTES
        ),
    )(*parts, small, *shares)


def exchange_kernel(arrays, pieces, *refs):
    shares, totals = refs[:arrays], refs[arrays : 2 * arrays]
    mine, theirs = refs[2 * arrays : 3 * arrays], refs[3 * arrays : 4 * arrays]
    send_sem, recv_sem = refs[4 * arrays :]
    peer = 1 - lax.axis_index("tensor")
    barrier = pltpu.get_barrier_semaphore()
    pl.semaphore_signal(barrier, inc=1, device_id={"tensor": peer}, device_id_type=MESH)
    pl.semaphore_wait(barrier, 1)
    copies = {}
    for k in range(arrays):
        size = shares[k].shape[0] // pieces[k]
        for piece in range(pieces[k]):
            at = pl.ds(piece * size, size)
            mine[k][at, :] = shares[k][at, :].astype(jnp.bfloat16)
            copies[k, piece] = pltpu.make_async_remote_copy(
                src_ref=mine[k].at[at],
                dst_ref=theirs[k].at[at],
                send_sem=send_sem.at[k, piece],
                recv_sem=recv_sem.at[k, piece],
                device_id={"tensor": peer},
                device_id_type=MESH,
            )
            copies[k, piece].start()
    for k in range(arrays):
        size = shares[k].shape[0] // pieces[k]
        for piece in range(pieces[k]):
            at = pl.ds(piece * size, size)
            copies[k, piece].wait()
            totals[k][at, :] = mine[k][at, :].astype(jnp.float32) + theirs[k][at, :].astype(
                jnp.float32
            )


def tensor_sum(shares, ways, collective_id):
    if ways != 2:
        return tuple(lax.psum(share, "tensor") for share in shares)
    arrays = len(shares)
    pieces = tuple(4 if share.shape[0] % 64 == 0 else 1 for share in shares)
    vmem = pl.BlockSpec(memory_space=pltpu.VMEM)
    buffers = [pltpu.VMEM(share.shape, jnp.bfloat16) for share in shares]
    return pl.pallas_call(
        partial(exchange_kernel, arrays, pieces),
        out_shape=tuple(jax.ShapeDtypeStruct(share.shape, jnp.float32) for share in shares),
        in_specs=[vmem] * arrays,
        out_specs=(vmem,) * arrays,
        scratch_shapes=buffers + buffers + [pltpu.SemaphoreType.DMA((arrays, 4))] * 2,
        compiler_params=pltpu.CompilerParams(
            collective_id=collective_id, has_side_effects=True, vmem_limit_bytes=VMEM_BYTES
        ),
    )(*shares)


def body(
    hidden_in,
    seq_lengths,
    norm_in,
    w_z,
    w_x,
    w_bc,
    w_dt,
    conv_x,
    conv_bc,
    head_params,
    w_out,
    w_q,
    key_weight,
    value_weight,
    w_o,
    norm_mlp,
    w_gate,
    w_up,
    w_down,
    cotangent,
):
    count = lax.axis_size("dp")
    ways = lax.axis_size("tensor")
    width_z, width_bc, width_dt = w_z.shape[1], w_bc.shape[1], w_dt.shape[1]
    width_q, width_k, width_o = w_q.shape[1], key_weight.shape[1], w_o.shape[0]
    width_ff = w_gate.shape[1]
    thin = jnp.concatenate([w_dt, norm_in[:, None], norm_mlp[:, None]], axis=1)
    thin = jnp.pad(thin, ((0, 0), (0, -thin.shape[1] % 128)))
    packed_in, packed_out, full_glu, down_t = gather_rows(
        (
            jnp.concatenate([w_z, w_x, w_bc, w_q, key_weight, value_weight, thin], axis=1),
            jnp.concatenate([w_out.T, w_o.T], axis=1),
            jnp.concatenate([w_gate, w_up], axis=1),
            w_down.T,
        ),
        count,
        0,
    )
    edges = [0]
    for width in (width_z, width_z, width_bc, width_q, width_k, width_k, width_dt):
        edges.append(edges[-1] + width)
    gain_in = packed_in[:, edges[7]]
    gain_mlp = packed_in[:, edges[7] + 1]
    inputs = hidden_in.astype(jnp.float32)
    count_of_rows = inputs.shape[0]
    segment, token_position, live_rows = layout(seq_lengths, count_of_rows)
    live_column = live_rows[:, None]
    row_index = jnp.arange(count_of_rows, dtype=jnp.int32)
    visible = (segment[:, None] == segment[None, :]) & (row_index[None, :] <= row_index[:, None])
    normed_full, norm_in_pull = jax.vjp(root_norm, inputs, gain_in.astype(jnp.float32))
    normalized_input = normed_full.astype(jnp.bfloat16)
    projected = product(normalized_input, packed_in)
    gate_ssm, conv_in, bc_raw, q_raw, k_raw, v_raw, step_raw = (
        projected[:, left:right] for left, right in zip(edges[:-1], edges[1:])
    )
    bc_act, bc_pull = jax.vjp(
        partial(causal_conv, segment=segment), bc_raw, conv_bc.astype(jnp.float32)
    )
    gated_full, mamba_pull = jax.vjp(
        partial(mamba_core, segment=segment),
        gate_ssm,
        conv_in,
        step_raw,
        conv_x.astype(jnp.float32),
        head_params,
        bc_act,
    )
    gated_out = gated_full.astype(jnp.bfloat16)
    query_heads = width_q // HEAD_WIDTH
    kv_heads = width_k // HEAD_WIDTH
    queries = rotary_embedding(
        q_raw.reshape(count_of_rows, query_heads, HEAD_WIDTH),
        token_position,
        1.0,
    ).astype(jnp.bfloat16)
    key_matrix_rows = rotary_embedding(
        k_raw.reshape(count_of_rows, kv_heads, HEAD_WIDTH),
        token_position,
        1.0,
    ).astype(jnp.bfloat16)
    value_matrix_rows = (
        v_raw.astype(jnp.bfloat16)
        .reshape(count_of_rows, kv_heads, HEAD_WIDTH)
    )
    attended_full, log_total = attend_forward(queries, key_matrix_rows, value_matrix_rows, visible)
    attended = attended_full.astype(jnp.bfloat16)
    mixed_in = jnp.concatenate([gated_out, attended], axis=1)
    (mixed_sum,) = tensor_sum((back_product(mixed_in, packed_out),), ways, 1)
    residual = inputs + live_column * mixed_sum
    normed_mlp_full, norm_mlp_pull = jax.vjp(root_norm, residual, gain_mlp.astype(jnp.float32))
    normed_mlp = normed_mlp_full.astype(jnp.bfloat16)
    glu_pre = product(normed_mlp, full_glu)
    gate_pre, up_pre = glu_pre[:, :width_ff], glu_pre[:, width_ff:]
    activated = (jax.nn.silu(gate_pre) * up_pre).astype(jnp.bfloat16)
    mlp_share = back_product(activated, down_t).astype(jnp.bfloat16)
    grad_out = cotangent.astype(jnp.float32)
    grad_mlp = (live_column * grad_out).astype(jnp.bfloat16)
    grad_act = product(grad_mlp, down_t)
    sigmoid_gate = jax.nn.sigmoid(gate_pre)
    grad_gate = (grad_act * up_pre * sigmoid_gate * (1.0 + gate_pre * (1.0 - sigmoid_gate))).astype(
        jnp.bfloat16
    )
    grad_up = (grad_act * jax.nn.silu(gate_pre)).astype(jnp.bfloat16)
    grad_glu = jnp.concatenate([grad_gate, grad_up], axis=1)
    part_down = rows_product(grad_mlp, activated).astype(jnp.bfloat16)
    part_glu = rows_product(normed_mlp, grad_glu).astype(jnp.bfloat16)
    (grad_normed_mlp,) = tensor_sum((back_product(grad_glu, full_glu),), ways, 3)
    grad_residual_norm, part_gain_mlp = norm_mlp_pull(grad_normed_mlp)
    grad_residual = grad_out + grad_residual_norm
    grad_mixed = (live_column * grad_residual).astype(jnp.bfloat16)
    grad_mixed_in = product(grad_mixed, packed_out)
    grad_gated = grad_mixed_in[:, :width_z]
    grad_attended = grad_mixed_in[:, width_z:].astype(jnp.bfloat16)
    part_out = rows_product(grad_mixed, mixed_in).astype(jnp.bfloat16)
    grad_queries, grad_keys, grad_values = attend_backward(
        queries, key_matrix_rows, value_matrix_rows, visible, log_total, grad_attended
    )
    grad_q = (
        rotary_embedding(grad_queries, token_position, -1.0)
        .reshape(count_of_rows, -1)
        .astype(jnp.bfloat16)
    )
    grad_k = (
        rotary_embedding(grad_keys, token_position, -1.0)
        .reshape(count_of_rows, -1)
        .astype(jnp.bfloat16)
    )
    grad_v = grad_values.reshape(count_of_rows, -1).astype(jnp.bfloat16)
    grad_gate_ssm, grad_conv_in, grad_step, part_conv_x, part_heads, bc_share = mamba_pull(
        grad_gated
    )
    bc_raw_share, conv_bc_share = bc_pull(bc_share)
    grad_projected = jnp.concatenate(
        [
            grad_gate_ssm.astype(jnp.bfloat16),
            grad_conv_in.astype(jnp.bfloat16),
            bc_raw_share.astype(jnp.bfloat16),
            grad_q,
            grad_k,
            grad_v,
            grad_step.astype(jnp.bfloat16),
            jnp.zeros((count_of_rows, packed_in.shape[1] - edges[7]), jnp.bfloat16),
        ],
        axis=1,
    )
    norm_share = back_product(grad_projected, packed_in).astype(jnp.bfloat16)
    _, gain_in_share = norm_in_pull(norm_share.astype(jnp.float32))
    part_in = rows_product(normalized_input, grad_projected).astype(jnp.bfloat16)
    conv_rows = conv_bc.shape[0]
    head_rows, head_count = head_params.shape
    model_width = inputs.shape[1]
    small = jnp.concatenate(
        [
            jnp.pad(conv_bc_share, ((0, 8 - conv_rows), (0, 0))),
            gain_in_share.reshape(8, model_width // 8),
            part_gain_mlp.reshape(8, model_width // 8),
            jnp.pad(part_conv_x, ((0, 8 - conv_rows), (0, 0))),
            jnp.pad(part_heads, ((0, 8 - head_rows), (0, -head_count % 128))),
        ],
        axis=1,
    )
    marks = [0]
    for width in (width_bc, model_width // 8, model_width // 8, width_z, head_count):
        marks.append(marks[-1] + width)
    sum_in, sum_out_o, sum_glu, sum_down, sum_small, mlp_out, grad_normed = scatter_rows(
        (part_in, part_out, part_glu, part_down),
        small,
        (mlp_share, norm_share),
        (edges[2], width_bc),
        marks[2],
        count,
        ways,
        5,
    )
    layer_out = residual + live_column * mlp_out
    grad_input_norm, _ = norm_in_pull(grad_normed)
    grad_in = grad_residual + grad_input_norm
    sum_z, sum_x, sum_bc, sum_q, sum_k, sum_v, sum_dt = (
        sum_in[:, left:right] for left, right in zip(edges[:-1], edges[1:])
    )
    sum_conv_bc, all_gain_in, all_gain_mlp, sum_conv_x, sum_heads = (
        sum_small[:, left:right] for left, right in zip(marks[:-1], marks[1:])
    )
    sum_conv_bc, sum_conv_x = sum_conv_bc[:conv_rows], sum_conv_x[:conv_rows]
    sum_heads = sum_heads[:head_rows]
    gain_size = norm_in.shape[0]
    gain_start = lax.axis_index("dp") * gain_size
    sum_gain_in, sum_gain_mlp = (
        lax.dynamic_slice_in_dim(gain.reshape(model_width), gain_start, gain_size)
        for gain in (all_gain_in, all_gain_mlp)
    )
    sum_out = sum_out_o[:, :width_z].T
    sum_o = sum_out_o[:, width_z:].T
    sum_gate, sum_up = sum_glu[:, :width_ff], sum_glu[:, width_ff:]
    sum_down = sum_down.T
    return (
        layer_out,
        grad_in,
        sum_gain_in,
        sum_z,
        sum_x,
        sum_bc,
        sum_dt,
        sum_conv_x,
        sum_conv_bc,
        sum_heads,
        sum_out,
        sum_q,
        sum_k,
        sum_v,
        sum_o,
        sum_gain_mlp,
        sum_gate,
        sum_up,
        sum_down,
    )


def solution(mesh):
    return jax.shard_map(
        body,
        mesh=mesh,
        in_specs=(
            P("dp", None),
            P("dp"),
            P("dp"),
            P("dp", "tensor"),
            P("dp", "tensor"),
            P("dp", None),
            P("dp", "tensor"),
            P(None, "tensor"),
            P(),
            P(None, "tensor"),
            P("tensor", "dp"),
            P("dp", "tensor"),
            P("dp", "tensor"),
            P("dp", "tensor"),
            P("tensor", "dp"),
            P("dp"),
            P("dp", "tensor"),
            P("dp", "tensor"),
            P("tensor", "dp"),
            P("dp", None),
        ),
        out_specs=(
            P("dp", None),
            P("dp", None),
            P("dp"),
            P("dp", "tensor"),
            P("dp", "tensor"),
            P("dp", None),
            P("dp", "tensor"),
            P(None, "tensor"),
            P(),
            P(None, "tensor"),
            P("tensor", "dp"),
            P("dp", "tensor"),
            P("dp", "tensor"),
            P("dp", "tensor"),
            P("tensor", "dp"),
            P("dp"),
            P("dp", "tensor"),
            P("dp", "tensor"),
            P("tensor", "dp"),
        ),
        check_vma=False,
    )
```

```python
from functools import partial

import jax
import jax.numpy as jnp
from jax import lax
from jax.experimental import pallas as pl
from jax.experimental.pallas import tpu as pltpu
from jax.sharding import PartitionSpec as P

HEAD_WIDTH = 64


EPSILON = 1e-05
ROTARY_BASE = 100000000000.0
MASKED = -1e30
EXACT_PRODUCT = lax.Precision.HIGHEST


def product(left_side, right_side):
    return jnp.dot(left_side, right_side, preferred_element_type=jnp.float32)


def rows_product(left_side, right_side):
    return lax.dot_general(
        left_side, right_side, (((0,), (0,)), ((), ())), preferred_element_type=jnp.float32
    )


def back_product(left_side, right_side):
    return lax.dot_general(
        left_side, right_side, (((1,), (1,)), ((), ())), preferred_element_type=jnp.float32
    )


def root_norm(values, scale_row):
    return (
        values * lax.rsqrt(jnp.mean(values * values, axis=-1, keepdims=True) + EPSILON) * scale_row
    )


def layout(lengths, count_of_rows):
    row_index = jnp.arange(count_of_rows, dtype=jnp.int32)
    seq_ends = jnp.cumsum(lengths)
    segment = jnp.sum((row_index[:, None] >= seq_ends[None, :]).astype(jnp.int32), axis=1)
    slot_index = jnp.arange(lengths.shape[0], dtype=jnp.int32)
    starts = jnp.sum(jnp.where(slot_index[None, :] < segment[:, None], lengths[None, :], 0), axis=1)
    live_rows = (row_index < seq_ends[-1]).astype(jnp.float32)
    return (segment, row_index - starts, live_rows)


def rotary_embedding(values, token_position, direction):
    half_width = values.shape[-1] // 2
    frequency = ROTARY_BASE ** (-jnp.arange(half_width, dtype=jnp.float32) / half_width)
    angles = token_position.astype(jnp.float32)[:, None] * frequency[None, :]
    cosine = jnp.cos(angles)[:, None, :]
    sine_part = direction * jnp.sin(angles)[:, None, :]
    first_half = values[..., :half_width]
    second_half = values[..., half_width:]
    return jnp.concatenate(
        [
            first_half * cosine - second_half * sine_part,
            second_half * cosine + first_half * sine_part,
        ],
        axis=-1,
    )


def causal_conv(values, taps_bias, segment):
    kernel_len = taps_bias.shape[0] - 1
    conv_sum = taps_bias[kernel_len][None, :] + taps_bias[kernel_len - 1][None, :] * values
    for offset in range(1, kernel_len):
        shifted = jnp.concatenate(
            [jnp.zeros((offset, values.shape[1]), values.dtype), values[:-offset]], axis=0
        )
        earlier = jnp.concatenate([jnp.full((offset,), -1, jnp.int32), segment[:-offset]], axis=0)
        same_doc = (earlier == segment).astype(values.dtype)[:, None]
        conv_sum = conv_sum + taps_bias[kernel_len - 1 - offset][None, :] * shifted * same_doc
    return jax.nn.silu(conv_sum)


def state_mix(mixer_in, bc_act, step_raw, head_params, segment):
    count_of_rows, head_count = step_raw.shape
    state_width = bc_act.shape[1] // 2
    inputs = mixer_in.reshape(count_of_rows, head_count, -1)
    decay_rate = jnp.exp(head_params[0])
    step_size = jax.nn.softplus(step_raw + head_params[1][None, :])
    log_decay = jnp.cumsum(-step_size * decay_rate[None, :], axis=0).T
    row_index = jnp.arange(count_of_rows, dtype=jnp.int32)
    visible = (segment[:, None] == segment[None, :]) & (row_index[None, :] <= row_index[:, None])
    log_gap = log_decay[:, :, None] - log_decay[:, None, :]
    decay_mat = jnp.exp(jnp.where(visible[None], log_gap, -jnp.inf))
    intersection = jnp.dot(
        bc_act[:, state_width:], bc_act[:, :state_width].T, precision=EXACT_PRODUCT
    )
    mixing = intersection[None] * decay_mat * step_size.T[:, None, :]
    result = jnp.einsum("hts,shp->thp", mixing, inputs, precision=EXACT_PRODUCT)
    result = result + head_params[2][None, :, None] * inputs
    return result.reshape(count_of_rows, -1)


def mamba_core(gate_ssm, conv_in, step_raw, conv_taps, head_params, bc_act, segment):
    mixer_in = causal_conv(conv_in, conv_taps, segment)
    return state_mix(mixer_in, bc_act, step_raw, head_params, segment) * jax.nn.silu(gate_ssm)


def attend_forward(queries, key_matrix_rows, value_matrix_rows, visible):
    count_of_rows, head_count, head_size = queries.shape
    kv_count = key_matrix_rows.shape[1]
    grouped = queries.reshape(count_of_rows, kv_count, head_count // kv_count, head_size)
    scores = jnp.einsum(
        "tkgd,skd->kgts", grouped, key_matrix_rows, preferred_element_type=jnp.float32
    )
    logits = jnp.where(visible[None, None], scores * head_size ** (-0.5), MASKED)
    largest = jnp.max(logits, axis=-1, keepdims=True)
    weights_exp = jnp.exp(logits - largest)
    totals = jnp.sum(weights_exp, axis=-1, keepdims=True)
    attention_weights = weights_exp / totals
    attended = jnp.einsum(
        "kgts,skd->tkgd",
        attention_weights.astype(jnp.bfloat16),
        value_matrix_rows,
        preferred_element_type=jnp.float32,
    )
    return (attended.reshape(count_of_rows, head_count * head_size), largest + jnp.log(totals))


def attend_backward(queries, key_matrix_rows, value_matrix_rows, visible, log_total, grad_attended):
    count_of_rows, head_count, head_size = queries.shape
    kv_count = key_matrix_rows.shape[1]
    grouped = queries.reshape(count_of_rows, kv_count, head_count // kv_count, head_size)
    grad_grouped = grad_attended.reshape(count_of_rows, kv_count, head_count // kv_count, head_size)
    scores = jnp.einsum(
        "tkgd,skd->kgts", grouped, key_matrix_rows, preferred_element_type=jnp.float32
    )
    logits = jnp.where(visible[None, None], scores * head_size ** (-0.5), MASKED)
    attention_weights = jnp.exp(logits - log_total)
    grad_weights = jnp.einsum(
        "tkgd,skd->kgts", grad_grouped, value_matrix_rows, preferred_element_type=jnp.float32
    )
    inner_sum = jnp.sum(attention_weights * grad_weights, axis=-1, keepdims=True)
    grad_scores = (attention_weights * (grad_weights - inner_sum) * head_size ** (-0.5)).astype(
        jnp.bfloat16
    )
    grad_queries = jnp.einsum(
        "kgts,skd->tkgd", grad_scores, key_matrix_rows, preferred_element_type=jnp.float32
    )
    grad_keys = jnp.einsum(
        "kgts,tkgd->skd", grad_scores, grouped, preferred_element_type=jnp.float32
    )
    grad_values = jnp.einsum(
        "kgts,tkgd->skd",
        attention_weights.astype(jnp.bfloat16),
        grad_grouped,
        preferred_element_type=jnp.float32,
    )
    return (grad_queries.reshape(count_of_rows, head_count, head_size), grad_keys, grad_values)


MESH = pl.DeviceIdType.MESH
VMEM_BYTES = 52 * 1024 * 1024
ADD_ROWS = 16


def place(count):
    me = lax.axis_index("dp")
    core = lax.rem(me, 2)
    column = lax.rem(lax.div(me, 2), 2)
    line = lax.div(me, 4)
    return me, line, column, core, count // 4


def dp_index(line, column, core):
    return (line * 2 + column) * 2 + core


def greet(peers, partner=None):
    barrier = pltpu.get_barrier_semaphore()
    if partner is not None:
        pl.semaphore_signal(barrier, inc=1, device_id={"tensor": partner}, device_id_type=MESH)
    for peer in peers:
        pl.semaphore_signal(barrier, inc=1, device_id={"dp": peer}, device_id_type=MESH)
    pl.semaphore_wait(barrier, len(peers) + (partner is not None))


def gather_kernel(count, arrays, *refs):
    shards, wholes = refs[:arrays], refs[arrays : 2 * arrays]
    own_sem, line_send, line_recv, side_send, side_recv, core_send, core_recv = refs[2 * arrays :]
    me, line, column, core, length = place(count)
    side = dp_index(line, 1 - column, core)
    sibling = dp_index(line, column, 1 - core)
    ahead = [dp_index(lax.rem(line + d, length), column, core) for d in range(1, length)]
    greet(ahead + [side, sibling])

    def rows(array, index):
        size = shards[array].shape[0]
        return wholes[array].at[pl.ds(pl.multiple_of(index * size, size), size)]

    hops = length - 1
    steps = [(hop, way) for hop in range(hops) for way in (0, 1)]
    slots = 1 + 2 * hops

    def slot(hop, way):
        return 1 + way * hops + hop

    def owner(hop, way):
        return line + 1 + hop if way else line - 1 - hop

    def arrives(hop, way):
        return owner(hop, way) < length if way else owner(hop, way) >= 0

    def has_next(way):
        return line > 0 if way else line < length - 1

    def remote(source, target, send_sem, recv_sem, peer):
        return pltpu.make_async_remote_copy(
            src_ref=source,
            dst_ref=target,
            send_sem=send_sem,
            recv_sem=recv_sem,
            device_id={"dp": peer},
            device_id_type=MESH,
        )

    def line_copy(k, hop, way, source, target):
        peer = dp_index(lax.rem(line + (hops if way else 1), length), column, core)
        at = slot(hop, way)
        return remote(source, target, line_send.at[k, at], line_recv.at[k, at], peer)

    def side_copy(k, at, source, target):
        return remote(source, target, side_send.at[k, at], side_recv.at[k, at], side)

    def core_copy(k, at, source, target):
        return remote(source, target, core_send.at[k, at], core_recv.at[k, at], sibling)

    own = []
    for k in range(arrays):
        mine = rows(k, me)
        side_copy(k, 0, shards[k], mine).start()
        for way in (0, 1):

            @pl.when(has_next(way))
            def _():
                line_copy(k, 0, way, shards[k], mine).start()

        core_copy(k, 0, shards[k], mine).start()
        copy = pltpu.make_async_copy(shards[k], mine, own_sem.at[k])
        copy.start()
        own.append(copy)

    def pass_side(k):
        block = rows(k, side)
        side_copy(k, 0, block, block).wait_recv()
        core_copy(k, slots, block, block).start()
        for hop, way in steps:

            @pl.when(arrives(hop, way))
            def _():
                at = slot(hop, way)
                block = rows(k, dp_index(owner(hop, way), 1 - column, core))
                side_copy(k, at, block, block).wait_recv()
                core_copy(k, slots + at, block, block).start()

    for k in range(arrays):
        for hop, way in steps:

            @pl.when(arrives(hop, way))
            def _():
                at = slot(hop, way)
                block = rows(k, dp_index(owner(hop, way), column, core))
                line_copy(k, hop, way, block, block).wait_recv()
                if hop + 1 < hops:

                    @pl.when(has_next(way))
                    def _():
                        line_copy(k, hop + 1, way, block, block).start()

                side_copy(k, at, block, block).start()
                core_copy(k, at, block, block).start()

        if k:
            pass_side(k - 1)
    pass_side(arrays - 1)
    for k in range(arrays):
        own[k].wait()
        mine, theirs = rows(k, me), rows(k, sibling)
        side_copy(k, 0, shards[k], mine).wait_send()
        core_copy(k, 0, shards[k], mine).wait_send()
        core_copy(k, 0, theirs, theirs).wait_recv()
        block = rows(k, side)
        core_copy(k, slots, block, block).wait()
        for way in (0, 1):

            @pl.when(has_next(way))
            def _():
                line_copy(k, 0, way, shards[k], mine).wait_send()

        for hop, way in steps:

            @pl.when(arrives(hop, way))
            def _():
                at = slot(hop, way)
                block = rows(k, dp_index(owner(hop, way), column, core))
                side_copy(k, at, block, block).wait_send()
                core_copy(k, at, block, block).wait()
                core_copy(k, slots + at, block, block).wait()
                if hop + 1 < hops:

                    @pl.when(has_next(way))
                    def _():
                        line_copy(k, hop + 1, way, block, block).wait_send()


def gather_rows(shards, count, collective_id):
    if shards[0].shape[0] % 16 or count % 4:
        return tuple(lax.all_gather(shard, "dp", axis=0, tiled=True) for shard in shards)
    arrays, length = len(shards), count // 4
    return pl.pallas_call(
        partial(gather_kernel, count, arrays),
        out_shape=tuple(
            jax.ShapeDtypeStruct((count * s.shape[0], s.shape[1]), s.dtype) for s in shards
        ),
        in_specs=[pl.BlockSpec(memory_space=pl.ANY)] * arrays,
        out_specs=(pl.BlockSpec(memory_space=pl.ANY),) * arrays,
        scratch_shapes=[pltpu.SemaphoreType.DMA((arrays,))]
        + [pltpu.SemaphoreType.DMA((arrays, 2 * length - 1))] * 4
        + [pltpu.SemaphoreType.DMA((arrays, 4 * length - 2))] * 2,
        compiler_params=pltpu.CompilerParams(collective_id=collective_id, has_side_effects=True),
    )(*shards)


def scatter_kernel(count, arrays, pairs, paired, paired_small, *refs):
    parts, small = refs[:arrays], refs[arrays]
    shares, refs = refs[arrays + 1 : arrays + 1 + pairs], refs[arrays + 1 + pairs :]
    sums, small_sum = refs[:arrays], refs[arrays]
    totals, rest = refs[arrays + 1 : arrays + 1 + pairs], refs[arrays + 1 + pairs :]
    theirs, rest = rest[:pairs], rest[pairs:]
    pair_in, pair_small, pair_send, pair_recv = rest[:4]
    rest = rest[4:]
    partner = 1 - lax.axis_index("tensor")
    from_core, from_side, from_line = (
        rest[:arrays],
        rest[arrays : 2 * arrays],
        rest[2 * arrays : 3 * arrays],
    )
    small_core, small_pair, small_side, small_line = rest[3 * arrays : 3 * arrays + 4]
    core_send, core_recv, side_send, side_recv, line_send, line_recv = rest[3 * arrays + 4 :]
    me, line, column, core, length = place(count)
    side = dp_index(line, 1 - column, core)
    sibling = dp_index(line, column, 1 - core)
    ahead = [dp_index(lax.rem(line + d, length), column, core) for d in range(1, length)]
    greet(ahead + [side, sibling], partner)

    def swap(source, target, index):
        copy = pltpu.make_async_remote_copy(
            src_ref=source,
            dst_ref=target,
            send_sem=pair_send.at[index],
            recv_sem=pair_recv.at[index],
            device_id={"tensor": partner},
            device_id_type=MESH,
        )
        copy.start()
        return copy

    def send(source, target, send_sem, recv_sem, peer):
        copy = pltpu.make_async_remote_copy(
            src_ref=source,
            dst_ref=target,
            send_sem=send_sem,
            recv_sem=recv_sem,
            device_id={"dp": peer},
            device_id_type=MESH,
        )
        copy.start()
        return copy

    def part_start(k, d, block_column, block_core):
        size = sums[k].shape[0]
        return pl.multiple_of(
            dp_index(lax.rem(line + d, length), block_column, block_core) * size, size
        )

    def add_into(target, terms, size):
        @pl.loop(0, size // ADD_ROWS)
        def _(step):
            shift = step * ADD_ROWS
            total = None
            for ref, start in terms:
                at = pl.ds(pl.multiple_of(start + shift, ADD_ROWS), ADD_ROWS)
                value = ref[at, :].astype(jnp.float32)
                total = value if total is None else total + value
            ref, start = target
            at = pl.ds(pl.multiple_of(start + shift, ADD_ROWS), ADD_ROWS)
            ref[at, :] = total.astype(ref.dtype)

    core_copies, side_copies, line_copies = {}, {}, {}
    last = arrays
    core_copies[last, 0] = send(
        small, small_core, core_send.at[last, 0], core_recv.at[last, 0], sibling
    )
    far_first = [(k, d) for k in range(arrays) for d in range(1, length)]
    far_first += [(k, 0) for k in range(arrays)]
    for other in (1, 0):
        for k, d in far_first:
            size = sums[k].shape[0]
            j = other * length + d
            block_column = 1 - column if other else column
            start = part_start(k, d, block_column, 1 - core)
            core_copies[k, j] = send(
                parts[k].at[pl.ds(start, size)],
                from_core[k].at[pl.ds(j * size, size)],
                core_send.at[k, j],
                core_recv.at[k, j],
                sibling,
            )
    pair_copies = [swap(shares[i], theirs[i], i) for i in range(pairs)]
    core_copies[last, 0].wait_recv()
    small_pair[...] = small[...] + small_core[...]
    side_copies[last, 0] = send(
        small_pair, small_side, side_send.at[last, 0], side_recv.at[last, 0], side
    )
    for k, d in far_first:
        size = sums[k].shape[0]
        j = length + d
        core_copies[k, j].wait_recv()
        mine = part_start(k, d, 1 - column, core)
        add_into((from_core[k], j * size), [(from_core[k], j * size), (parts[k], mine)], size)
        side_copies[k, d] = send(
            from_core[k].at[pl.ds(j * size, size)],
            from_side[k].at[pl.ds(d * size, size)],
            side_send.at[k, d],
            side_recv.at[k, d],
            side,
        )
    side_copies[last, 0].wait_recv()
    small_line[line] = small_pair[...] + small_side[...]
    for d in range(1, length):
        line_copies[last, d] = send(
            small_line.at[line],
            small_line.at[line],
            line_send.at[last, d],
            line_recv.at[last, d],
            ahead[d - 1],
        )
    for k, d in far_first:
        size = sums[k].shape[0]
        core_copies[k, d].wait_recv()
        side_copies[k, d].wait_recv()
        if d:
            mine = part_start(k, d, column, core)
            terms = [
                (from_side[k], d * size),
                (from_core[k], d * size),
                (parts[k], mine),
            ]
            add_into((from_side[k], d * size), terms, size)
            line_copies[k, d] = send(
                from_side[k].at[pl.ds(d * size, size)],
                from_line[k].at[pl.ds((d - 1) * size, size)],
                line_send.at[k, d],
                line_recv.at[k, d],
                ahead[d - 1],
            )
    for i in range(pairs):
        pair_copies[i].wait()

        @pl.loop(0, shares[i].shape[0] // ADD_ROWS)
        def _(step):
            at = pl.ds(pl.multiple_of(step * ADD_ROWS, ADD_ROWS), ADD_ROWS)
            totals[i][at, :] = shares[i][at, :].astype(jnp.float32) + theirs[i][at, :].astype(
                jnp.float32
            )

    for d in range(1, length):
        line_copies[last, d].wait_recv()
    total = small_line[0]
    for position in range(1, length):
        total = total + small_line[position]
    small_sum[...] = total
    small_pairs = small_sum.at[:, pl.ds(0, paired_small)]
    swap_small = swap(small_pairs, pair_small, pairs)
    for k in range(arrays):
        size = sums[k].shape[0]
        terms = [
            (from_side[k], 0),
            (from_core[k], 0),
            (parts[k], part_start(k, 0, column, core)),
        ]
        for d in range(1, length):
            line_copies[k, d].wait_recv()
            terms.append((from_line[k], (d - 1) * size))
        add_into((sums[k], 0), terms, size)
        if k == 0:
            in_pairs = sums[0].at[:, pl.ds(paired[0], paired[1])]
            swap_in = swap(in_pairs, pair_in, pairs + 1)
    swap_small.wait()
    small_pairs[...] = small_pairs[...] + pair_small[...]
    swap_in.wait()
    in_pairs[...] = in_pairs[...] + pair_in[...]
    for copies in (core_copies, side_copies, line_copies):
        for copy in copies.values():
            copy.wait_send()


def scatter_rows(parts, small, shares, paired, paired_small, count, ways, collective_id):
    size = parts[0].shape[0] // count
    if size % 16 or count % 4 or ways != 2:
        sums = [
            lax.psum_scatter(part.astype(jnp.float32), "dp", scatter_dimension=0, tiled=True)
            for part in parts
        ]
        left, right = paired[0], paired[0] + paired[1]
        middle = lax.psum(sums[0][:, left:right], "tensor")
        sums[0] = jnp.concatenate([sums[0][:, :left], middle, sums[0][:, right:]], axis=1)
        small = lax.psum(small, "dp")
        both = lax.psum(small[:, :paired_small], "tensor")
        small = jnp.concatenate([both, small[:, paired_small:]], axis=1)
        totals = [lax.psum(share, "tensor").astype(jnp.float32) for share in shares]
        return (*sums, small, *totals)
    arrays, pairs, length = len(parts), len(shares), count // 4
    vmem = pl.BlockSpec(memory_space=pltpu.VMEM)
    widths = [part.shape[1] for part in parts]
    received = [
        pltpu.VMEM((blocks * size, width), jnp.bfloat16)
        for blocks in (2 * length, length, length - 1)
        for width in widths
    ]
    return pl.pallas_call(
        partial(scatter_kernel, count, arrays, pairs, paired, paired_small),
        out_shape=tuple(jax.ShapeDtypeStruct((size, width), jnp.float32) for width in widths)
        + (jax.ShapeDtypeStruct(small.shape, jnp.float32),)
        + tuple(jax.ShapeDtypeStruct(share.shape, jnp.float32) for share in shares),
        in_specs=[vmem] * (arrays + 1 + pairs),
        out_specs=(vmem,) * (arrays + 1 + pairs),
        scratch_shapes=[pltpu.VMEM(share.shape, share.dtype) for share in shares]
        + [
            pltpu.VMEM((size, paired[1]), jnp.float32),
            pltpu.VMEM((small.shape[0], paired_small), jnp.float32),
        ]
        + [pltpu.SemaphoreType.DMA((pairs + 2,))] * 2
        + received
        + [pltpu.VMEM(small.shape, jnp.float32)] * 3
        + [pltpu.VMEM((length,) + small.shape, jnp.float32)]
        + [pltpu.SemaphoreType.DMA((arrays + 1, 2 * length))] * 2
        + [pltpu.SemaphoreType.DMA((arrays + 1, length))] * 4,
        compiler_params=pltpu.CompilerParams(
            collective_id=collective_id, has_side_effects=True, vmem_limit_bytes=VMEM_BYTES
        ),
    )(*parts, small, *shares)


def exchange_kernel(arrays, pieces, *refs):
    shares, totals = refs[:arrays], refs[arrays : 2 * arrays]
    mine, theirs = refs[2 * arrays : 3 * arrays], refs[3 * arrays : 4 * arrays]
    send_sem, recv_sem = refs[4 * arrays :]
    peer = 1 - lax.axis_index("tensor")
    barrier = pltpu.get_barrier_semaphore()
    pl.semaphore_signal(barrier, inc=1, device_id={"tensor": peer}, device_id_type=MESH)
    pl.semaphore_wait(barrier, 1)
    copies = {}
    for k in range(arrays):
        size = shares[k].shape[0] // pieces[k]
        for piece in range(pieces[k]):
            at = pl.ds(piece * size, size)
            mine[k][at, :] = shares[k][at, :].astype(jnp.bfloat16)
            copies[k, piece] = pltpu.make_async_remote_copy(
                src_ref=mine[k].at[at],
                dst_ref=theirs[k].at[at],
                send_sem=send_sem.at[k, piece],
                recv_sem=recv_sem.at[k, piece],
                device_id={"tensor": peer},
                device_id_type=MESH,
            )
            copies[k, piece].start()
    for k in range(arrays):
        size = shares[k].shape[0] // pieces[k]
        for piece in range(pieces[k]):
            at = pl.ds(piece * size, size)
            copies[k, piece].wait()
            totals[k][at, :] = mine[k][at, :].astype(jnp.float32) + theirs[k][at, :].astype(
                jnp.float32
            )


def tensor_sum(shares, ways, collective_id):
    if ways != 2:
        return tuple(lax.psum(share, "tensor") for share in shares)
    arrays = len(shares)
    pieces = tuple(4 if share.shape[0] % 64 == 0 else 1 for share in shares)
    vmem = pl.BlockSpec(memory_space=pltpu.VMEM)
    buffers = [pltpu.VMEM(share.shape, jnp.bfloat16) for share in shares]
    return pl.pallas_call(
        partial(exchange_kernel, arrays, pieces),
        out_shape=tuple(jax.ShapeDtypeStruct(share.shape, jnp.float32) for share in shares),
        in_specs=[vmem] * arrays,
        out_specs=(vmem,) * arrays,
        scratch_shapes=buffers + buffers + [pltpu.SemaphoreType.DMA((arrays, 4))] * 2,
        compiler_params=pltpu.CompilerParams(
            collective_id=collective_id, has_side_effects=True, vmem_limit_bytes=VMEM_BYTES
        ),
    )(*shares)


def body(
    hidden_in,
    seq_lengths,
    norm_in,
    w_z,
    w_x,
    w_bc,
    w_dt,
    conv_x,
    conv_bc,
    head_params,
    w_out,
    w_q,
    key_weight,
    value_weight,
    w_o,
    norm_mlp,
    w_gate,
    w_up,
    w_down,
    cotangent,
):
    count = lax.axis_size("dp")
    ways = lax.axis_size("tensor")
    width_z, width_bc, width_dt = w_z.shape[1], w_bc.shape[1], w_dt.shape[1]
    width_q, width_k, width_o = w_q.shape[1], key_weight.shape[1], w_o.shape[0]
    width_ff = w_gate.shape[1]
    thin = jnp.concatenate([w_dt, norm_in[:, None], norm_mlp[:, None]], axis=1)
    thin = jnp.pad(thin, ((0, 0), (0, -thin.shape[1] % 128)))
    packed_in, packed_out, full_glu, down_t = gather_rows(
        (
            jnp.concatenate([w_z, w_x, w_bc, w_q, key_weight, value_weight, thin], axis=1),
            jnp.concatenate([w_out.T, w_o.T], axis=1),
            jnp.concatenate([w_gate, w_up], axis=1),
            w_down.T,
        ),
        count,
        0,
    )
    edges = [0]
    for width in (width_z, width_z, width_bc, width_q, width_k, width_k, width_dt):
        edges.append(edges[-1] + width)
    gain_in = packed_in[:, edges[7]]
    gain_mlp = packed_in[:, edges[7] + 1]
    inputs = hidden_in.astype(jnp.float32)
    count_of_rows = inputs.shape[0]
    segment, token_position, live_rows = layout(seq_lengths, count_of_rows)
    live_column = live_rows[:, None]
    row_index = jnp.arange(count_of_rows, dtype=jnp.int32)
    visible = (segment[:, None] == segment[None, :]) & (row_index[None, :] <= row_index[:, None])
    normed_full, norm_in_pull = jax.vjp(root_norm, inputs, gain_in.astype(jnp.float32))
    normalized_input = normed_full.astype(jnp.bfloat16)
    projected = product(normalized_input, packed_in)
    gate_ssm, conv_in, bc_raw, q_raw, k_raw, v_raw, step_raw = (
        projected[:, left:right] for left, right in zip(edges[:-1], edges[1:])
    )
    bc_act, bc_pull = jax.vjp(
        partial(causal_conv, segment=segment), bc_raw, conv_bc.astype(jnp.float32)
    )
    gated_full, mamba_pull = jax.vjp(
        partial(mamba_core, segment=segment),
        gate_ssm,
        conv_in,
        step_raw,
        conv_x.astype(jnp.float32),
        head_params,
        bc_act,
    )
    gated_out = gated_full.astype(jnp.bfloat16)
    query_heads = width_q // HEAD_WIDTH
    kv_heads = width_k // HEAD_WIDTH
    queries = rotary_embedding(
        q_raw.reshape(count_of_rows, query_heads, HEAD_WIDTH),
        token_position,
        1.0,
    ).astype(jnp.bfloat16)
    key_matrix_rows = rotary_embedding(
        k_raw.reshape(count_of_rows, kv_heads, HEAD_WIDTH),
        token_position,
        1.0,
    ).astype(jnp.bfloat16)
    value_matrix_rows = (
        v_raw.astype(jnp.bfloat16)
        .reshape(count_of_rows, kv_heads, HEAD_WIDTH)
    )
    attended_full, log_total = attend_forward(queries, key_matrix_rows, value_matrix_rows, visible)
    attended = attended_full.astype(jnp.bfloat16)
    mixed_in = jnp.concatenate([gated_out, attended], axis=1)
    (mixed_sum,) = tensor_sum((back_product(mixed_in, packed_out),), ways, 1)
    residual = inputs + live_column * mixed_sum
    normed_mlp_full, norm_mlp_pull = jax.vjp(root_norm, residual, gain_mlp.astype(jnp.float32))
    normed_mlp = normed_mlp_full.astype(jnp.bfloat16)
    glu_pre = product(normed_mlp, full_glu)
    gate_pre, up_pre = glu_pre[:, :width_ff], glu_pre[:, width_ff:]
    activated = (jax.nn.silu(gate_pre) * up_pre).astype(jnp.bfloat16)
    mlp_share = back_product(activated, down_t).astype(jnp.bfloat16)
    grad_out = cotangent.astype(jnp.float32)
    grad_mlp = (live_column * grad_out).astype(jnp.bfloat16)
    grad_act = product(grad_mlp, down_t)
    sigmoid_gate = jax.nn.sigmoid(gate_pre)
    grad_gate = (grad_act * up_pre * sigmoid_gate * (1.0 + gate_pre * (1.0 - sigmoid_gate))).astype(
        jnp.bfloat16
    )
    grad_up = (grad_act * jax.nn.silu(gate_pre)).astype(jnp.bfloat16)
    grad_glu = jnp.concatenate([grad_gate, grad_up], axis=1)
    part_down = rows_product(grad_mlp, activated).astype(jnp.bfloat16)
    part_glu = rows_product(normed_mlp, grad_glu).astype(jnp.bfloat16)
    (grad_normed_mlp,) = tensor_sum((back_product(grad_glu, full_glu),), ways, 3)
    grad_residual_norm, part_gain_mlp = norm_mlp_pull(grad_normed_mlp)
    grad_residual = grad_out + grad_residual_norm
    grad_mixed = (live_column * grad_residual).astype(jnp.bfloat16)
    grad_mixed_in = product(grad_mixed, packed_out)
    grad_gated = grad_mixed_in[:, :width_z]
    grad_attended = grad_mixed_in[:, width_z:].astype(jnp.bfloat16)
    part_out = rows_product(grad_mixed, mixed_in).astype(jnp.bfloat16)
    grad_queries, grad_keys, grad_values = attend_backward(
        queries, key_matrix_rows, value_matrix_rows, visible, log_total, grad_attended
    )
    grad_q = (
        rotary_embedding(grad_queries, token_position, -1.0)
        .reshape(count_of_rows, -1)
        .astype(jnp.bfloat16)
    )
    grad_k = (
        rotary_embedding(grad_keys, token_position, -1.0)
        .reshape(count_of_rows, -1)
        .astype(jnp.bfloat16)
    )
    grad_v = grad_values.reshape(count_of_rows, -1).astype(jnp.bfloat16)
    grad_gate_ssm, grad_conv_in, grad_step, part_conv_x, part_heads, bc_share = mamba_pull(
        grad_gated
    )
    bc_raw_share, conv_bc_share = bc_pull(bc_share)
    grad_projected = jnp.concatenate(
        [
            grad_gate_ssm.astype(jnp.bfloat16),
            grad_conv_in.astype(jnp.bfloat16),
            bc_raw_share.astype(jnp.bfloat16),
            grad_q,
            grad_k,
            grad_v,
            grad_step.astype(jnp.bfloat16),
            jnp.zeros((count_of_rows, packed_in.shape[1] - edges[7]), jnp.bfloat16),
        ],
        axis=1,
    )
    norm_share = back_product(grad_projected, packed_in).astype(jnp.bfloat16)
    _, gain_in_share = norm_in_pull(norm_share.astype(jnp.float32))
    part_in = rows_product(normalized_input, grad_projected).astype(jnp.bfloat16)
    conv_rows = conv_bc.shape[0]
    head_rows, head_count = head_params.shape
    model_width = inputs.shape[1]
    small = jnp.concatenate(
        [
            jnp.pad(conv_bc_share, ((0, 8 - conv_rows), (0, 0))),
            gain_in_share.reshape(8, model_width // 8),
            part_gain_mlp.reshape(8, model_width // 8),
            jnp.pad(part_conv_x, ((0, 8 - conv_rows), (0, 0))),
            jnp.pad(part_heads, ((0, 8 - head_rows), (0, -head_count % 128))),
        ],
        axis=1,
    )
    marks = [0]
    for width in (width_bc, model_width // 8, model_width // 8, width_z, head_count):
        marks.append(marks[-1] + width)
    sum_in, sum_out_o, sum_glu, sum_down, sum_small, mlp_out, grad_normed = scatter_rows(
        (part_in, part_out, part_glu, part_down),
        small,
        (mlp_share, norm_share),
        (edges[2], width_bc),
        marks[2],
        count,
        ways,
        5,
    )
    layer_out = residual + live_column * mlp_out
    grad_input_norm, _ = norm_in_pull(grad_normed)
    grad_in = grad_residual + grad_input_norm
    sum_z, sum_x, sum_bc, sum_q, sum_k, sum_v, sum_dt = (
        sum_in[:, left:right] for left, right in zip(edges[:-1], edges[1:])
    )
    sum_conv_bc, all_gain_in, all_gain_mlp, sum_conv_x, sum_heads = (
        sum_small[:, left:right] for left, right in zip(marks[:-1], marks[1:])
    )
    sum_conv_bc, sum_conv_x = sum_conv_bc[:conv_rows], sum_conv_x[:conv_rows]
    sum_heads = sum_heads[:head_rows]
    gain_size = norm_in.shape[0]
    gain_start = lax.axis_index("dp") * gain_size
    sum_gain_in, sum_gain_mlp = (
        lax.dynamic_slice_in_dim(gain.reshape(model_width), gain_start, gain_size)
        for gain in (all_gain_in, all_gain_mlp)
    )
    sum_out = sum_out_o[:, :width_z].T
    sum_o = sum_out_o[:, width_z:].T
    sum_gate, sum_up = sum_glu[:, :width_ff], sum_glu[:, width_ff:]
    sum_down = sum_down.T
    return (
        layer_out,
        grad_in,
        sum_gain_in,
        sum_z,
        sum_x,
        sum_bc,
        sum_dt,
        sum_conv_x,
        sum_conv_bc,
        sum_heads,
        sum_out,
        sum_q,
        sum_k,
        sum_v,
        sum_o,
        sum_gain_mlp,
        sum_gate,
        sum_up,
        sum_down,
    )


def solution(mesh):
    return jax.shard_map(
        body,
        mesh=mesh,
        in_specs=(
            P("dp", None),
            P("dp"),
            P("dp"),
            P("dp", "tensor"),
            P("dp", "tensor"),
            P("dp", None),
            P("dp", "tensor"),
            P(None, "tensor"),
            P(),
            P(None, "tensor"),
            P("tensor", "dp"),
            P("dp", "tensor"),
            P("dp", "tensor"),
            P("dp", "tensor"),
            P("tensor", "dp"),
            P("dp"),
            P("dp", "tensor"),
            P("dp", "tensor"),
            P("tensor", "dp"),
            P("dp", None),
        ),
        out_specs=(
            P("dp", None),
            P("dp", None),
            P("dp"),
            P("dp", "tensor"),
            P("dp", "tensor"),
            P("dp", None),
            P("dp", "tensor"),
            P(None, "tensor"),
            P(),
            P(None, "tensor"),
            P("tensor", "dp"),
            P("dp", "tensor"),
            P("dp", "tensor"),
            P("dp", "tensor"),
            P("tensor", "dp"),
            P("dp"),
            P("dp", "tensor"),
            P("dp", "tensor"),
            P("tensor", "dp"),
        ),
        check_vma=False,
    )
```
